32 devices in a mesh: row: 8 (over y, x, core), col: 4 (over z).
Axes of the slice: x: 2, y: 2, z: 4, core: 2. Of those that a mesh axis runs over, the one named last changes fastest.
Arguments:
- telemetry: int32 [4096, 64], P(('col', 'row')), may hold values from -127 to 127
- scales: int32 [4096], P(('col', 'row')), may hold values from 1 to 4
- bands: int32 [2, 2], replicated, may hold values from 256 to 4096
- noise: float32 [4096], P('row'), may hold values from 0.5 to 2
- start: bfloat16 [4096, 64], P(('col', 'row')), may hold values from -6 to 6
- target: bfloat16 [4096, 64], P('row'), may hold values from -6 to 6
Outputs:
- first: float32 [4096, 64], P('row')
- second: float32 [4096, 64], P('row')
The draws below stay inside these ranges and needn't reach their ends.
All inputs are finite; a program needn't handle non-finite values.
Results may differ from the reference program's by a relative error of at most 0.0023.
Values may be sent and summed in bfloat16 or wider, within the bound.
No kernel may reach another device: no remote copies, remote signals or barrier semaphores. Data moves between devices by JAX's collectives and lax.ppermute only.
A program may use at most 128 MiB of HBM per device.

```python
import math
import jax
import jax.numpy as jnp
from jax import lax

SUBAP = 2048
FRAMES = 64
PANEL = 64
M = 4096
SENSORS = 2


def with_ends(entries, stream_key, low, top_value):
    dims = entries.shape
    index_at = [jax.random.randint(jax.random.fold_in(stream_key, axis), (), 0, dims[axis]) for axis in range(len(dims))]
    entries = entries.at[tuple(index_at)].set(low)
    longest = dims.index(max(dims))
    index_at[longest] = (index_at[longest] + 1) % dims[longest]
    return entries.at[tuple(index_at)].set(top_value)


def block_scale(own_key, dims, pieces, smallest, high):
    factor_of, own = 1.0, jax.random.fold_in(own_key, 6)
    for position, parts in pieces:
        draws = jnp.exp(jax.random.uniform(jax.random.fold_in(own, position), (parts,), jnp.float32, smallest / len(pieces), high / len(pieces)))
        factor_of = factor_of * jnp.repeat(draws, dims[position] // parts).reshape([-1 if axis == position else 1 for axis in range(len(dims))])
    return factor_of


def normal_values(rng, extent, spread, bound, shards=(), kind=jnp.bfloat16):
    array = spread * jax.random.normal(rng, extent, jnp.float32)
    if shards:
        array = array * block_scale(rng, extent, shards, -0.22, 0.18)
    return jnp.clip(array, -bound, bound).astype(kind)


def setup_inputs(seed: int = 0) -> dict:
    splits = jax.random.split(jax.random.key(seed), 7)
    return {
        "telemetry": with_ends(jax.random.randint(splits[0], (M, FRAMES), -127, 128), jax.random.fold_in(splits[0], 1), -127, 127).astype(jnp.int32),
        "scales": with_ends(jax.random.randint(splits[1], (M,), 1, 5), jax.random.fold_in(splits[1], 1), 1, 4).astype(jnp.int32),
        "bands": with_ends(jax.random.randint(splits[2], (SENSORS, SENSORS), SUBAP // 8, 2 * SUBAP + 1), jax.random.fold_in(splits[2], 1), SUBAP // 8, 2 * SUBAP).astype(jnp.int32),
        "noise": jnp.clip(jnp.exp(math.log(2.0) - 1.3862944 * jax.random.uniform(splits[3], (M,), jnp.float32) ** block_scale(splits[3], (M,), ((0, 8),), -0.2, 0.2)), 0.5, 2.0),
        "start": normal_values(splits[4], (M, PANEL), 1.0, 6.0, ((0, 32),)),
        "target": normal_values(splits[5], (M, PANEL), 1.0, 6.0, ((0, 8),)),
    }


damping = 0.4


def reference(telemetry, scales, bands, noise, start, target):
    norm_count = jnp.float32(M // 4)
    slopes = (telemetry.astype(jnp.float32) * scales.astype(jnp.float32)[:, None] / 128.0).astype(jnp.bfloat16)
    slope_f = slopes.astype(jnp.float32)
    weight = damping / (jnp.sum(slope_f * slope_f, axis=1) / norm_count + noise)
    count = bands.shape[0]
    index = jnp.arange(count, dtype=jnp.int32)
    sym = jnp.where(index[:, None] <= index[None, :], bands, bands.T).astype(jnp.float32)
    cols_all = jnp.arange(M, dtype=jnp.int32)
    col_pos = (cols_all % SUBAP).astype(jnp.float32)

    def apply(panel):
        def one(block_id):
            first_row = (block_id * SUBAP).astype(jnp.int32)
            rows = lax.dynamic_slice_in_dim(slope_f, first_row, SUBAP, 0)
            raw = jnp.dot(rows, slope_f.T, precision=lax.Precision.HIGHEST) / norm_count
            row_ids = first_row + jnp.arange(SUBAP, dtype=jnp.int32)
            band = sym[block_id][cols_all // SUBAP]
            dist = jnp.abs((row_ids % SUBAP).astype(jnp.float32)[:, None] - col_pos[None, :])
            taper = jnp.maximum(0.0, 1.0 - dist / band[None, :])
            row_noise = lax.dynamic_slice_in_dim(noise, first_row, SUBAP, 0)
            diag = jnp.where(row_ids[:, None] == cols_all[None, :], row_noise[:, None], jnp.float32(0.0))
            entry = (taper * raw + diag).astype(jnp.bfloat16)
            return jnp.dot(entry, panel, preferred_element_type=jnp.float32)

        out = lax.map(one, jnp.arange(M // SUBAP, dtype=jnp.int32))
        return out.reshape(M, panel.shape[1])

    target_f = target.astype(jnp.float32)
    product0 = apply(start)
    first = start.astype(jnp.float32) + weight[:, None] * (target_f - product0)
    product1 = apply(first.astype(jnp.bfloat16))
    second = first + weight[:, None] * (target_f - product1)
    return first, second
```

```python
import functools
import math

import jax
import jax.numpy as jnp
from jax import lax
from jax.experimental import pallas as pl
from jax.experimental.pallas import tpu as pltpu
from jax.sharding import PartitionSpec as P

SUBAP = 2048


damping = 0.4


def from_root(block, axis, holder):
    block = jnp.where(lax.axis_index(axis) == holder, block, jnp.zeros_like(block))
    return lax.psum(block, axis)


def tiled_plan(telemetry, scales, bands, noise, start, target):
    frame_count = telemetry.shape[1]
    row_count = lax.axis_size("row")
    col_count = lax.axis_size("col")
    ratio = row_count // col_count
    row_id = lax.axis_index("row")
    col_id = lax.axis_index("col")
    order_total = telemetry.shape[0] * row_count * col_count
    norm_count = jnp.float32(order_total // 4)
    slopes = (telemetry.astype(jnp.float32) * scales.astype(jnp.float32)[:, None] / 128.0).astype(
        jnp.bfloat16
    )
    joined = jnp.concatenate([slopes, start], axis=1)
    col_joined = lax.all_gather(joined, "row", axis=0, tiled=True)
    col_width = col_joined.shape[0]
    row_height = col_width // ratio
    half = lax.dynamic_slice_in_dim(col_joined, row_id % ratio * row_height, row_height, 0)
    row_joined = from_root(half, "col", row_id // ratio)
    row_slopes = row_joined[:, :frame_count]
    row_start = row_joined[:, frame_count:]
    col_slopes = col_joined[:, :frame_count]
    col_start = col_joined[:, frame_count:]
    panel_width = col_start.shape[1]
    row_f = row_slopes.astype(jnp.float32)
    weight = damping / (jnp.sum(row_f * row_f, axis=1) / norm_count + noise)
    count = bands.shape[0]
    index = jnp.arange(count, dtype=jnp.int32)
    sym = jnp.where(index[:, None] <= index[None, :], bands, bands.T).astype(jnp.float32)
    row_ids = row_id * row_height + jnp.arange(row_height, dtype=jnp.int32)
    onehot = (row_ids[:, None] // SUBAP == index[None, :]).astype(jnp.float32)
    row_band = jnp.dot(onehot, sym, precision=lax.Precision.HIGHEST)
    row_pos = (row_ids % SUBAP).astype(jnp.float32)
    width = math.gcd(math.gcd(col_width, 512), SUBAP)
    nblocks = col_width // width

    def build(step, carry):
        tile, acc = carry
        offset = step * width
        cols = lax.dynamic_slice_in_dim(col_slopes, offset, width, 0)
        raw = (
            lax.dot_general(
                row_slopes, cols, (((1,), (1,)), ((), ())), preferred_element_type=jnp.float32
            )
            / norm_count
        )
        col_ids = col_id * col_width + offset + jnp.arange(width, dtype=jnp.int32)
        band = lax.dynamic_slice_in_dim(row_band, (col_id * col_width + offset) // SUBAP, 1, 1)
        dist = jnp.abs(row_pos[:, None] - (col_ids % SUBAP).astype(jnp.float32)[None, :])
        taper = jnp.maximum(0.0, 1.0 - dist / band)
        diag = jnp.where(row_ids[:, None] == col_ids[None, :], noise[:, None], jnp.float32(0.0))
        entry = (taper * raw + diag).astype(jnp.bfloat16)
        tile = lax.dynamic_update_slice_in_dim(tile, entry, offset, 1)
        return (tile, acc)

    tile_init = jnp.zeros((row_height, col_width), jnp.bfloat16)
    acc_init = jnp.zeros((row_height, panel_width), jnp.float32)
    tile, acc = lax.fori_loop(0, nblocks, build, (tile_init, acc_init))
    product0 = jnp.dot(tile, col_start, preferred_element_type=jnp.float32)
    target_f = target.astype(jnp.float32)

    def refine(current, product):
        share = lax.psum_scatter(product, "col", scatter_dimension=0, tiled=True)
        share_rows = row_height // col_count
        begin = col_id * share_rows
        cur_part = lax.dynamic_slice_in_dim(current, begin, share_rows, 0)
        tgt_part = lax.dynamic_slice_in_dim(target_f, begin, share_rows, 0)
        wgt_part = lax.dynamic_slice_in_dim(weight, begin, share_rows, 0)
        updated = cur_part + wgt_part[:, None] * (tgt_part - share)
        return lax.all_gather(updated, "col", axis=0, tiled=True)

    first = refine(row_start.astype(jnp.float32), product0)
    first_low = first.astype(jnp.bfloat16)
    pieces = [from_root(first_low, "row", col_id * ratio + offset_q) for offset_q in range(ratio)]
    col_first = jnp.concatenate(pieces, axis=0)
    product1 = jnp.dot(tile, col_first, preferred_element_type=jnp.float32)
    second = refine(first, product1)
    return (first, second)


EDGE = 256


def first_kernel(
    sizes, ids, rates, mine, other, tile, low, first, weight, whole, noise_all
):
    rows_n, cols_n, chunk, height, panel, norm_count, hops = sizes
    order = rows_n * cols_n * chunk
    half = rows_n // 2
    col_id, row_id = ids[0], ids[1]
    core = row_id % 2
    for pos in range(half):
        for slot in range(cols_n):
            home = ((hops[slot] ^ col_id) * rows_n + 2 * pos + core) * chunk
            away = ((hops[slot] ^ col_id) * rows_n + 2 * pos + 1 - core) * chunk
            part = pl.ds(slot * chunk, chunk)
            whole[pl.ds(pl.multiple_of(home, chunk), chunk), :] = mine[pos, part, :]
            whole[pl.ds(pl.multiple_of(away, chunk), chunk), :] = other[pos, part, :]
    pieces = height // 128
    scale = jnp.float32(1.0 / norm_count)
    lanes = lax.broadcasted_iota(jnp.int32, (EDGE, 128), 1)
    ramp_r = lax.broadcasted_iota(jnp.int32, (EDGE, EDGE), 0)
    ramp_c = lax.broadcasted_iota(jnp.int32, (EDGE, EDGE), 1)
    own = row_id // 2
    parts = height // EDGE

    def block(step, _):
        pos = (own + 1 + step // parts) % half
        piece = step % parts
        base = (2 * pos + core) * height + piece * EDGE
        sensor = base // SUBAP
        place = base % SUBAP
        rows = whole[pl.ds(pl.multiple_of(base, EDGE), EDGE), :]
        only_s = jnp.where(lanes >= panel, rows, jnp.zeros_like(rows))
        ramp = (ramp_r - ramp_c).astype(jnp.float32)
        into = pl.ds(pl.multiple_of(piece * EDGE, EDGE), EDGE)
        for col in range(order // EDGE):
            cols = whole[pl.ds(col * EDGE, EDGE), :]
            raw = lax.dot_general(
                only_s, cols, (((1,), (1,)), ((), ())), preferred_element_type=jnp.float32
            )
            rate = rates[sensor, col * EDGE // SUBAP]
            gap = (place - col * EDGE % SUBAP).astype(jnp.float32)
            taper = jnp.maximum(0.0, scale - jnp.abs(ramp + gap) * (rate * scale))
            tile[into, pl.ds(col * EDGE, EDGE)] = (taper * raw).astype(jnp.bfloat16)
        cols = whole[pl.ds(pl.multiple_of(base, EDGE), EDGE), :]
        raw = lax.dot_general(
            only_s, cols, (((1,), (1,)), ((), ())), preferred_element_type=jnp.float32
        )
        planes = mine[pos, pl.ds(cols_n * chunk + height // 2, 16), :].astype(jnp.float32)
        noises = planes[0:pieces] + planes[pieces : 2 * pieces] + planes[2 * pieces : 3 * pieces]
        noise_all[0:pieces, :] = noises
        line = jnp.concatenate(
            [noise_all[pl.ds(piece * (EDGE // 128) + k, 1), :] for k in range(EDGE // 128)], axis=1
        )
        taper = jnp.maximum(0.0, scale - jnp.abs(ramp) * (rates[sensor, sensor] * scale))
        diag = jnp.where(ramp_r == ramp_c, line, 0.0)
        tile[into, pl.ds(pl.multiple_of(base, EDGE), EDGE)] = (taper * raw + diag).astype(jnp.bfloat16)
        bottom = jnp.sum(jnp.where(ramp_r == ramp_c, raw * scale + line, 0.0), axis=1, keepdims=True)
        wgt = damping / bottom
        product = jnp.dot(tile[into, :], whole[...], preferred_element_type=jnp.float32)
        pair = mine[pos, pl.ds(cols_n * chunk, height // 2), :]
        side = jnp.where(piece * EDGE < height // 2, pair[:, 0:panel], pair[:, panel:])
        goal = side.astype(jnp.float32)
        new = rows[:, 0:panel].astype(jnp.float32) + wgt * (goal - product[:, 0:panel])
        low[pos, into, :] = new.astype(jnp.bfloat16)
        first[into, :] = new
        weight[into, :] = jnp.broadcast_to(wgt, (EDGE, panel))
        return 0

    lax.fori_loop(0, half * parts, block, 0)


def second_kernel(sizes, ids, tile, home, away, first, weight, target, second):
    rows_n, cols_n, chunk, height, panel, norm_count, hops = sizes
    core = ids[1] % 2
    total = jnp.zeros((height, panel), jnp.float32)
    for pos in range(rows_n // 2):
        near = pl.multiple_of((2 * pos + core) * height, height)
        far = pl.multiple_of((2 * pos + 1 - core) * height, height)
        total += jnp.dot(tile[:, pl.ds(near, height)], home[pos], preferred_element_type=jnp.float32)
        total += jnp.dot(tile[:, pl.ds(far, height)], away[pos], preferred_element_type=jnp.float32)
    second[...] = first[...] + weight[...] * (target[...].astype(jnp.float32) - total)


def flip(block, axis, bit):
    size = lax.axis_size(axis)
    return lax.ppermute(block, axis, [(i, i ^ bit) for i in range(size)])


def gathered_plan(telemetry, scales, bands, noise, start, target):
    rows_n = lax.axis_size("row")
    cols_n = lax.axis_size("col")
    chunk, frames = telemetry.shape
    height, panel = target.shape
    order = chunk * rows_n * cols_n
    half = rows_n // 2
    ids = jnp.stack([lax.axis_index("col"), lax.axis_index("row")]).astype(jnp.int32)
    count = bands.shape[0]
    index = jnp.arange(count, dtype=jnp.int32)
    sym = jnp.where(index[:, None] <= index[None, :], bands, bands.T).astype(jnp.float32)
    rates = 1.0 / sym
    slopes = (telemetry.astype(jnp.float32) * scales.astype(jnp.float32)[:, None] / 128.0).astype(
        jnp.bfloat16
    )
    block = jnp.concatenate([start, slopes], axis=1)
    hops = (0,)
    bit = cols_n // 2
    while bit:
        block = jnp.concatenate([block, flip(block, "col", bit)], axis=0)
        hops = hops + tuple(hop ^ bit for hop in hops)
        bit //= 2
    sizes = (rows_n, cols_n, chunk, height, panel, float(order // 4), hops)
    pair = jnp.concatenate([target[: height // 2], target[height // 2 :]], axis=1)
    high = lax.reduce_precision(noise, 8, 7)
    rest = noise - high
    middle = lax.reduce_precision(rest, 8, 7)
    planes = jnp.concatenate([high, middle, rest - middle]).astype(jnp.bfloat16).reshape(-1, 128)
    planes = jnp.pad(planes, ((0, 16 - planes.shape[0]), (0, 0)))
    payload = jnp.concatenate([block, pair, planes], axis=0)
    groups = [list(range(k, rows_n, 2)) for k in range(2)]
    mine = lax.all_gather(payload, "row", axis=0, axis_index_groups=groups)
    other = flip(mine, "row", 1)
    vmem = pl.BlockSpec(memory_space=pltpu.VMEM)
    smem = pl.BlockSpec(memory_space=pltpu.SMEM)
    tile, low, first, weight = pl.pallas_call(
        functools.partial(first_kernel, sizes),
        out_shape=(
            jax.ShapeDtypeStruct((height, order), jnp.bfloat16),
            jax.ShapeDtypeStruct((half, height, panel), jnp.bfloat16),
            jax.ShapeDtypeStruct((height, panel), jnp.float32),
            jax.ShapeDtypeStruct((height, panel), jnp.float32),
        ),
        in_specs=[smem, smem, vmem, vmem],
        out_specs=(vmem, vmem, vmem, vmem),
        scratch_shapes=[
            pltpu.VMEM((order, 128), jnp.bfloat16),
            pltpu.VMEM((8, 128), jnp.float32),
        ],
        compiler_params=pltpu.CompilerParams(vmem_limit_bytes=40 * 1024 * 1024),
        name="first_pass",
    )(ids, rates, mine, other)
    away = flip(low, "row", 1)
    second = pl.pallas_call(
        functools.partial(second_kernel, sizes),
        out_shape=jax.ShapeDtypeStruct((height, panel), jnp.float32),
        in_specs=[smem, vmem, vmem, vmem, vmem, vmem, vmem],
        out_specs=vmem,
        compiler_params=pltpu.CompilerParams(vmem_limit_bytes=40 * 1024 * 1024),
        name="second_pass",
    )(ids, tile, low, away, first, weight, target)
    return (first, second)


def power_of_two(number):
    return number > 0 and number & (number - 1) == 0


def fits(mesh, telemetry, target):
    rows_n, cols_n = mesh.shape["row"], mesh.shape["col"]
    order, frames = telemetry.shape
    panel = target.shape[1]
    height = order // rows_n
    return (
        power_of_two(rows_n)
        and power_of_two(cols_n)
        and rows_n >= 2
        and frames == panel == 64
        and order % SUBAP == 0
        and SUBAP % height == 0
        and height == 2 * EDGE
        and order // (rows_n * cols_n) % 16 == 0
        and order <= 2 * SUBAP
    )


def solution(mesh):
    def program(telemetry, scales, bands, noise, start, target):
        plan = gathered_plan if fits(mesh, telemetry, target) else tiled_plan
        return jax.shard_map(
            plan,
            mesh=mesh,
            in_specs=(
                P(("col", "row"), None),
                P(("col", "row")),
                P(),
                P("row"),
                P(("col", "row"), None),
                P("row", None),
            ),
            out_specs=(P("row", None), P("row", None)),
            check_vma=False,
        )(telemetry, scales, bands, noise, start, target)

    return program
```

```python
import functools
import math

import jax
import jax.numpy as jnp
from jax import lax
from jax.experimental import pallas as pl
from jax.experimental.pallas import tpu as pltpu
from jax.sharding import PartitionSpec as P

SUBAP = 2048


damping = 0.4


def from_root(block, axis, holder):
    block = jnp.where(lax.axis_index(axis) == holder, block, jnp.zeros_like(block))
    return lax.psum(block, axis)


def tiled_plan(telemetry, scales, bands, noise, start, target):
    frame_count = telemetry.shape[1]
    row_count = lax.axis_size("row")
    col_count = lax.axis_size("col")
    ratio = row_count // col_count
    row_id = lax.axis_index("row")
    col_id = lax.axis_index("col")
    order_total = telemetry.shape[0] * row_count * col_count
    norm_count = jnp.float32(order_total // 4)
    slopes = (telemetry.astype(jnp.float32) * scales.astype(jnp.float32)[:, None] / 128.0).astype(
        jnp.bfloat16
    )
    joined = jnp.concatenate([slopes, start], axis=1)
    col_joined = lax.all_gather(joined, "row", axis=0, tiled=True)
    col_width = col_joined.shape[0]
    row_height = col_width // ratio
    half = lax.dynamic_slice_in_dim(col_joined, row_id % ratio * row_height, row_height, 0)
    row_joined = from_root(half, "col", row_id // ratio)
    row_slopes = row_joined[:, :frame_count]
    row_start = row_joined[:, frame_count:]
    col_slopes = col_joined[:, :frame_count]
    col_start = col_joined[:, frame_count:]
    panel_width = col_start.shape[1]
    row_f = row_slopes.astype(jnp.float32)
    weight = damping / (jnp.sum(row_f * row_f, axis=1) / norm_count + noise)
    count = bands.shape[0]
    index = jnp.arange(count, dtype=jnp.int32)
    sym = jnp.where(index[:, None] <= index[None, :], bands, bands.T).astype(jnp.float32)
    row_ids = row_id * row_height + jnp.arange(row_height, dtype=jnp.int32)
    onehot = (row_ids[:, None] // SUBAP == index[None, :]).astype(jnp.float32)
    row_band = jnp.dot(onehot, sym, precision=lax.Precision.HIGHEST)
    row_pos = (row_ids % SUBAP).astype(jnp.float32)
    width = math.gcd(math.gcd(col_width, 512), SUBAP)
    nblocks = col_width // width

    def build(step, carry):
        tile, acc = carry
        offset = step * width
        cols = lax.dynamic_slice_in_dim(col_slopes, offset, width, 0)
        raw = (
            lax.dot_general(
                row_slopes, cols, (((1,), (1,)), ((), ())), preferred_element_type=jnp.float32
            )
            / norm_count
        )
        col_ids = col_id * col_width + offset + jnp.arange(width, dtype=jnp.int32)
        band = lax.dynamic_slice_in_dim(row_band, (col_id * col_width + offset) // SUBAP, 1, 1)
        dist = jnp.abs(row_pos[:, None] - (col_ids % SUBAP).astype(jnp.float32)[None, :])
        taper = jnp.maximum(0.0, 1.0 - dist / band)
        diag = jnp.where(row_ids[:, None] == col_ids[None, :], noise[:, None], jnp.float32(0.0))
        entry = (taper * raw + diag).astype(jnp.bfloat16)
        tile = lax.dynamic_update_slice_in_dim(tile, entry, offset, 1)
        return (tile, acc)

    tile_init = jnp.zeros((row_height, col_width), jnp.bfloat16)
    acc_init = jnp.zeros((row_height, panel_width), jnp.float32)
    tile, acc = lax.fori_loop(0, nblocks, build, (tile_init, acc_init))
    product0 = jnp.dot(tile, col_start, preferred_element_type=jnp.float32)
    target_f = target.astype(jnp.float32)

    def refine(current, product):
        share = lax.psum_scatter(product, "col", scatter_dimension=0, tiled=True)
        share_rows = row_height // col_count
        begin = col_id * share_rows
        cur_part = lax.dynamic_slice_in_dim(current, begin, share_rows, 0)
        tgt_part = lax.dynamic_slice_in_dim(target_f, begin, share_rows, 0)
        wgt_part = lax.dynamic_slice_in_dim(weight, begin, share_rows, 0)
        updated = cur_part + wgt_part[:, None] * (tgt_part - share)
        return lax.all_gather(updated, "col", axis=0, tiled=True)

    first = refine(row_start.astype(jnp.float32), product0)
    first_low = first.astype(jnp.bfloat16)
    pieces = [from_root(first_low, "row", col_id * ratio + offset_q) for offset_q in range(ratio)]
    col_first = jnp.concatenate(pieces, axis=0)
    product1 = jnp.dot(tile, col_first, preferred_element_type=jnp.float32)
    second = refine(first, product1)
    return (first, second)


EDGE = 256
STEP = 128
PAD = 384


def prepare_kernel(telemetry, scales, start, target, noise, block, side):
    panel, chunk = start.shape
    slopes = telemetry[...].astype(jnp.float32) * scales[...].astype(jnp.float32) / 128.0
    block[0:panel, :] = start[...]
    block[panel:, :] = slopes.astype(jnp.bfloat16)
    pieces = target.shape[1] // STEP
    for piece in range(pieces):
        part = slice(piece * STEP, (piece + 1) * STEP)
        side[piece * panel : (piece + 1) * panel, :] = target[:, part]
    rest = jnp.concatenate(
        [noise[:, piece * STEP : (piece + 1) * STEP] for piece in range(pieces)], axis=0
    )
    planes = []
    for _ in range(3):
        plane = rest.astype(jnp.bfloat16).astype(jnp.float32)
        rest = rest - plane
        planes.append(plane)
    planes.append(jnp.zeros_like(rest))
    side[pieces * panel :, :] = jnp.concatenate(planes, axis=0).astype(jnp.bfloat16)


def spot(row):
    return row + row // SUBAP * (2 * PAD) + PAD


def column(ref, begin, width, rows=slice(None)):
    return ref[rows, pl.ds(pl.multiple_of(begin, STEP), width)]


def moments(panel_ref, flat, sums):
    panel = 64
    local = (lax.broadcasted_iota(jnp.int32, (panel, STEP), 1) - STEP // 2).astype(jnp.float32)
    for sensor in range(sums.shape[0]):
        plain = jnp.zeros((panel, 128), jnp.float32)
        moved = jnp.zeros((panel, 128), jnp.float32)
        for t in range(SUBAP // STEP):
            sums[sensor, t, 0:panel, :] = plain
            sums[sensor, t, panel:, :] = moved
            begin = sensor * (SUBAP + 2 * PAD) + PAD + t * STEP
            x = panel_ref[0:panel, begin : begin + STEP]
            xq = (x.astype(jnp.float32) * local).astype(jnp.bfloat16)
            both = jnp.dot(
                jnp.concatenate([x, xq], axis=0),
                flat[begin : begin + STEP, :],
                preferred_element_type=jnp.float32,
            )
            plain = plain + both[0:panel]
            moved = moved + (both[panel:] + both[0:panel] * float(t * STEP + STEP // 2))
        sums[sensor, SUBAP // STEP, 0:panel, :] = plain
        sums[sensor, SUBAP // STEP, panel:, :] = moved


def multiply(base, norm_count, bands, panel_ref, wide, flat, sums, lines, accs):
    panel = 64
    scale = 1.0 / norm_count
    sensors = sums.shape[0]
    sensor = base // SUBAP
    count = len(lines)
    rows_i = lax.broadcasted_iota(jnp.int32, (PAD, EDGE), 0)
    cols_i = lax.broadcasted_iota(jnp.int32, (PAD, EDGE), 1)
    ramp = (rows_i - cols_i).astype(jnp.float32)
    square = ramp[0:EDGE]
    eye = rows_i[0:EDGE] == cols_i[0:EDGE]
    local = (lax.broadcasted_iota(jnp.int32, (panel, EDGE), 1) - EDGE // 2).astype(jnp.float32)
    slopes = []
    for k in range(count):
        both = column(wide, spot(base + k * EDGE), EDGE)
        keep = lax.broadcasted_iota(jnp.int32, both.shape, 0) >= panel
        slopes.append(jnp.where(keep, both, jnp.zeros_like(both)))
    place = [(base + k * EDGE) % SUBAP for k in range(count)]
    width = [bands[jnp.minimum(sensor, b), jnp.maximum(sensor, b)] for b in range(sensors)]
    low = [[jnp.minimum((p - w) // STEP * STEP, p - PAD) for p in place] for w in width]
    high = [[jnp.maximum((p + w) // STEP * STEP, p + EDGE) for p in place] for w in width]

    def raw_at(k, begin, size):
        return jnp.dot(
            flat[pl.ds(pl.multiple_of(begin, STEP), size), :],
            slopes[k],
            preferred_element_type=jnp.float32,
        )

    def carry(k, begin, size, entry):
        return jnp.dot(
            column(panel_ref, begin, size, slice(0, panel)), entry, preferred_element_type=jnp.float32
        )

    for k in range(count):
        total = jnp.zeros((panel, EDGE), jnp.float32)
        near = jnp.zeros((panel, 128), jnp.float32)
        tilt = jnp.zeros((panel, 128), jnp.float32)
        middle = (place[k] + EDGE // 2).astype(jnp.float32)
        for b in range(sensors):
            rate = 1.0 / jnp.full((panel, 128), width[b].astype(jnp.float32))
            at = [
                jnp.maximum(low[b][k] + PAD, 0) // STEP,
                place[k] // STEP,
                (place[k] + EDGE) // STEP,
                jnp.minimum(high[b][k], SUBAP) // STEP,
            ]
            zero = [sums[b, t, 0:panel, :] for t in at]
            one = [sums[b, t, panel:, :] for t in at]
            left, right = zero[1] - zero[0], zero[3] - zero[2]
            left_q, right_q = one[1] - one[0], one[3] - one[2]
            near += left + right + rate * ((left_q - middle * left) - (right_q - middle * right))
            tilt += rate * (right - left)
            begin = b * (SUBAP + 2 * PAD) + PAD + place[k]
            fall = (1.0 / jnp.full((EDGE, EDGE), width[b].astype(jnp.float32))) * scale
            taper = jnp.maximum(0.0, scale - jnp.abs(square) * fall)
            same = (sensor == b).astype(jnp.float32)
            entry = taper * raw_at(k, begin, EDGE) + jnp.where(eye, lines[k] * same, 0.0)
            total += carry(k, begin, EDGE, entry.astype(jnp.bfloat16))
        mix = jnp.concatenate([near, tilt], axis=0) * scale
        mix_high = mix.astype(jnp.bfloat16)
        mix_low = (mix - mix_high.astype(jnp.float32)).astype(jnp.bfloat16)
        far = jnp.dot(mix_high, slopes[k], preferred_element_type=jnp.float32)
        far += jnp.dot(mix_low, slopes[k], preferred_element_type=jnp.float32)
        accs[k][...] = total + far[0:panel] + local * far[panel:]

    for b in range(sensors):
        for side in (0, 1):
            begins = low[b] if side == 0 else high[b]
            wanted = low[b][count - 1] + PAD > 0 if side == 0 else high[b][0] < SUBAP

            @pl.when(wanted)
            def _(b=b, side=side, begins=begins):
                fall = (1.0 / jnp.full((PAD, EDGE), width[b].astype(jnp.float32))) * scale
                for k in range(count):
                    inside = jnp.maximum(begins[k], -PAD) if side == 0 else jnp.minimum(begins[k], SUBAP)
                    begin = b * (SUBAP + 2 * PAD) + PAD + inside
                    gap = (inside - place[k]).astype(jnp.float32)
                    away = ramp + gap
                    if side == 0:
                        taper = jnp.maximum(0.0, scale + away * fall)
                    else:
                        taper = jnp.maximum(0.0, scale - away * fall)
                    entry = (taper * raw_at(k, begin, PAD)).astype(jnp.bfloat16)
                    accs[k][...] += carry(k, begin, PAD, entry)


def first_kernel(sizes, ids, bands, mine, other, wide, flat, low, first, weight, sums, *accs):
    rows_n, cols_n, chunk, height, panel, norm_count, hops = sizes
    half = rows_n // 2
    col_id, row_id = ids[0], ids[1]
    core = row_id % 2
    own = row_id // 2
    stride = SUBAP + 2 * PAD
    for sensor in range(sums.shape[0]):
        for begin in (sensor * stride, sensor * stride + PAD + SUBAP):
            wide[:, begin : begin + PAD] = jnp.zeros((2 * panel, PAD), jnp.bfloat16)
            flat[begin : begin + PAD, :] = jnp.zeros((PAD, 2 * panel), jnp.bfloat16)
    for pos in range(half):
        for slot in range(cols_n):
            for source, parity in ((mine, core), (other, 1 - core)):
                row = ((hops[slot] ^ col_id) * rows_n + 2 * pos + parity) * chunk
                place = pl.multiple_of(spot(row), STEP)
                part = source[pos, slot * chunk : (slot + 1) * chunk, :]
                wide[:, pl.ds(place, chunk)] = part
                flat[pl.ds(place, chunk), :] = part.T
    moments(wide, flat, sums)
    pieces = height // STEP
    each = EDGE // STEP
    tail = cols_n * chunk

    def block(step, _):
        pos = (own + 1 + step) % half
        base = (2 * pos + core) * height
        planes = mine[pos, tail + pieces * panel : tail + pieces * panel + 16, :].astype(jnp.float32)
        noise = planes[0:pieces] + planes[pieces : 2 * pieces] + planes[2 * pieces : 3 * pieces]
        lines = []
        for k in range(height // EDGE):
            lines.append(
                jnp.concatenate([noise[t : t + 1] for t in range(k * each, (k + 1) * each)], axis=1)
            )
        multiply(base, norm_count, bands, wide, wide, flat, sums, lines, accs)
        for k in range(height // EDGE):
            both = column(wide, spot(base + k * EDGE), EDGE).astype(jnp.float32)
            power = jnp.sum(both[panel:] * both[panel:], axis=0, keepdims=True)
            wgt = damping / (power / norm_count + lines[k])
            goal = jnp.concatenate(
                [
                    mine[pos, tail + t * panel : tail + (t + 1) * panel, :]
                    for t in range(k * each, (k + 1) * each)
                ],
                axis=1,
            ).astype(jnp.float32)
            new = both[0:panel] + wgt * (goal - accs[k][...])
            part = slice(k * EDGE, (k + 1) * EDGE)
            first[:, part] = new
            weight[:, part] = jnp.broadcast_to(wgt, (8, EDGE))
            into = pl.multiple_of(pos * height + k * EDGE, EDGE)
            low[:, pl.ds(into, EDGE)] = new.astype(jnp.bfloat16)
        return 0

    lax.fori_loop(0, half, block, 0)


def second_kernel(sizes, ids, bands, wide, flat, home, away, first, weight, target, noise, second, new, sums, *accs):
    rows_n, cols_n, chunk, height, panel, norm_count, hops = sizes
    core = ids[1] % 2
    stride = SUBAP + 2 * PAD
    for sensor in range(sums.shape[0]):
        for begin in (sensor * stride, sensor * stride + PAD + SUBAP):
            new[:, begin : begin + PAD] = jnp.zeros((panel, PAD), jnp.bfloat16)
    for pos in range(rows_n // 2):
        for source, parity in ((home, core), (away, 1 - core)):
            place = pl.multiple_of(spot((2 * pos + parity) * height), STEP)
            new[:, pl.ds(place, height)] = source[:, pos * height : (pos + 1) * height]
    moments(new, flat, sums)
    parts = [slice(k * EDGE, (k + 1) * EDGE) for k in range(height // EDGE)]
    lines = [noise[:, part] for part in parts]
    multiply(ids[1] * height, norm_count, bands, new, wide, flat, sums, lines, accs)
    for k, part in enumerate(parts):
        goal = target[:, part].astype(jnp.float32)
        second[:, part] = first[:, part] + weight[0:1, part] * (goal - accs[k][...])


def flip(block, axis, bit):
    size = lax.axis_size(axis)
    return lax.ppermute(block, axis, [(i, i ^ bit) for i in range(size)])


def gathered_plan(telemetry, scales, bands, noise, start, target):
    rows_n = lax.axis_size("row")
    cols_n = lax.axis_size("col")
    chunk, frames = telemetry.shape
    height, panel = target.shape
    order = chunk * rows_n * cols_n
    sensors = order // SUBAP
    padded = order + 2 * PAD * sensors
    half = rows_n // 2
    ids = jnp.stack([lax.axis_index("col"), lax.axis_index("row")]).astype(jnp.int32)
    vmem = pl.BlockSpec(memory_space=pltpu.VMEM)
    smem = pl.BlockSpec(memory_space=pltpu.SMEM)
    params = pltpu.CompilerParams(vmem_limit_bytes=24 * 1024 * 1024)
    noise = noise.reshape(1, height)
    target = target.T
    block, side = pl.pallas_call(
        prepare_kernel,
        out_shape=(
            jax.ShapeDtypeStruct((2 * panel, chunk), jnp.bfloat16),
            jax.ShapeDtypeStruct((height // STEP * panel + 16, 128), jnp.bfloat16),
        ),
        in_specs=[vmem] * 5,
        out_specs=(vmem, vmem),
        compiler_params=params,
        name="prepare",
    )(telemetry.T, scales.reshape(1, chunk), start.T, target, noise)
    hops = (0,)
    bit = cols_n // 2
    while bit:
        block = jnp.concatenate([block, flip(block, "col", bit)], axis=0)
        hops = hops + tuple(hop ^ bit for hop in hops)
        bit //= 2
    sizes = (rows_n, cols_n, chunk, height, panel, float(order // 4), hops)
    payload = jnp.concatenate([block, side], axis=0)
    groups = [list(range(k, rows_n, 2)) for k in range(2)]
    mine = lax.all_gather(payload, "row", axis=0, axis_index_groups=groups)
    other = flip(mine, "row", 1)
    accs = [pltpu.VMEM((panel, EDGE), jnp.float32)] * (height // EDGE)
    sums = pltpu.VMEM((sensors, SUBAP // STEP + 1, 2 * panel, 128), jnp.float32)
    wide, flat, low, first, weight = pl.pallas_call(
        functools.partial(first_kernel, sizes),
        out_shape=(
            jax.ShapeDtypeStruct((2 * panel, padded), jnp.bfloat16),
            jax.ShapeDtypeStruct((padded, 2 * panel), jnp.bfloat16),
            jax.ShapeDtypeStruct((panel, half * height), jnp.bfloat16),
            jax.ShapeDtypeStruct((panel, height), jnp.float32),
            jax.ShapeDtypeStruct((8, height), jnp.float32),
        ),
        in_specs=[smem, smem, vmem, vmem],
        out_specs=(vmem,) * 5,
        scratch_shapes=[sums] + accs,
        compiler_params=params,
        name="first_pass",
    )(ids, bands, mine, other)
    away = flip(low, "row", 1)
    second = pl.pallas_call(
        functools.partial(second_kernel, sizes),
        out_shape=jax.ShapeDtypeStruct((panel, height), jnp.float32),
        in_specs=[smem, smem] + [vmem] * 8,
        out_specs=vmem,
        scratch_shapes=[pltpu.VMEM((panel, padded), jnp.bfloat16), sums] + accs,
        compiler_params=params,
        name="second_pass",
    )(ids, bands, wide, flat, low, away, first, weight, target, noise)
    return (first.T, second.T)


def power_of_two(number):
    return number > 0 and number & (number - 1) == 0


def fits(mesh, telemetry, target):
    rows_n, cols_n = mesh.shape["row"], mesh.shape["col"]
    order, frames = telemetry.shape
    panel = target.shape[1]
    height = order // rows_n
    return (
        power_of_two(rows_n)
        and power_of_two(cols_n)
        and rows_n >= 2
        and frames == panel == 64
        and order % SUBAP == 0
        and SUBAP % height == 0
        and height == 2 * EDGE
        and order // (rows_n * cols_n) == STEP
        and order <= 2 * SUBAP
    )


def solution(mesh):
    def program(telemetry, scales, bands, noise, start, target):
        plan = gathered_plan if fits(mesh, telemetry, target) else tiled_plan
        return jax.shard_map(
            plan,
            mesh=mesh,
            in_specs=(
                P(("col", "row"), None),
                P(("col", "row")),
                P(),
                P("row"),
                P(("col", "row"), None),
                P("row", None),
            ),
            out_specs=(P("row", None), P("row", None)),
            check_vma=False,
        )(telemetry, scales, bands, noise, start, target)

    return program
```

```python
import functools
import math

import jax
import jax.numpy as jnp
from jax import lax
from jax.experimental import pallas as pl
from jax.experimental.pallas import tpu as pltpu
from jax.sharding import PartitionSpec as P

SUBAP = 2048


damping = 0.4


def from_root(block, axis, holder):
    block = jnp.where(lax.axis_index(axis) == holder, block, jnp.zeros_like(block))
    return lax.psum(block, axis)


def tiled_plan(telemetry, scales, bands, noise, start, target):
    frame_count = telemetry.shape[1]
    row_count = lax.axis_size("row")
    col_count = lax.axis_size("col")
    ratio = row_count // col_count
    row_id = lax.axis_index("row")
    col_id = lax.axis_index("col")
    order_total = telemetry.shape[0] * row_count * col_count
    norm_count = jnp.float32(order_total // 4)
    slopes = (telemetry.astype(jnp.float32) * scales.astype(jnp.float32)[:, None] / 128.0).astype(
        jnp.bfloat16
    )
    joined = jnp.concatenate([slopes, start], axis=1)
    col_joined = lax.all_gather(joined, "row", axis=0, tiled=True)
    col_width = col_joined.shape[0]
    row_height = col_width // ratio
    half = lax.dynamic_slice_in_dim(col_joined, row_id % ratio * row_height, row_height, 0)
    row_joined = from_root(half, "col", row_id // ratio)
    row_slopes = row_joined[:, :frame_count]
    row_start = row_joined[:, frame_count:]
    col_slopes = col_joined[:, :frame_count]
    col_start = col_joined[:, frame_count:]
    panel_width = col_start.shape[1]
    row_f = row_slopes.astype(jnp.float32)
    weight = damping / (jnp.sum(row_f * row_f, axis=1) / norm_count + noise)
    count = bands.shape[0]
    index = jnp.arange(count, dtype=jnp.int32)
    sym = jnp.where(index[:, None] <= index[None, :], bands, bands.T).astype(jnp.float32)
    row_ids = row_id * row_height + jnp.arange(row_height, dtype=jnp.int32)
    onehot = (row_ids[:, None] // SUBAP == index[None, :]).astype(jnp.float32)
    row_band = jnp.dot(onehot, sym, precision=lax.Precision.HIGHEST)
    row_pos = (row_ids % SUBAP).astype(jnp.float32)
    width = math.gcd(math.gcd(col_width, 512), SUBAP)
    nblocks = col_width // width

    def build(step, carry):
        tile, acc = carry
        offset = step * width
        cols = lax.dynamic_slice_in_dim(col_slopes, offset, width, 0)
        raw = (
            lax.dot_general(
                row_slopes, cols, (((1,), (1,)), ((), ())), preferred_element_type=jnp.float32
            )
            / norm_count
        )
        col_ids = col_id * col_width + offset + jnp.arange(width, dtype=jnp.int32)
        band = lax.dynamic_slice_in_dim(row_band, (col_id * col_width + offset) // SUBAP, 1, 1)
        dist = jnp.abs(row_pos[:, None] - (col_ids % SUBAP).astype(jnp.float32)[None, :])
        taper = jnp.maximum(0.0, 1.0 - dist / band)
        diag = jnp.where(row_ids[:, None] == col_ids[None, :], noise[:, None], jnp.float32(0.0))
        entry = (taper * raw + diag).astype(jnp.bfloat16)
        tile = lax.dynamic_update_slice_in_dim(tile, entry, offset, 1)
        return (tile, acc)

    tile_init = jnp.zeros((row_height, col_width), jnp.bfloat16)
    acc_init = jnp.zeros((row_height, panel_width), jnp.float32)
    tile, acc = lax.fori_loop(0, nblocks, build, (tile_init, acc_init))
    product0 = jnp.dot(tile, col_start, preferred_element_type=jnp.float32)
    target_f = target.astype(jnp.float32)

    def refine(current, product):
        share = lax.psum_scatter(product, "col", scatter_dimension=0, tiled=True)
        share_rows = row_height // col_count
        begin = col_id * share_rows
        cur_part = lax.dynamic_slice_in_dim(current, begin, share_rows, 0)
        tgt_part = lax.dynamic_slice_in_dim(target_f, begin, share_rows, 0)
        wgt_part = lax.dynamic_slice_in_dim(weight, begin, share_rows, 0)
        updated = cur_part + wgt_part[:, None] * (tgt_part - share)
        return lax.all_gather(updated, "col", axis=0, tiled=True)

    first = refine(row_start.astype(jnp.float32), product0)
    first_low = first.astype(jnp.bfloat16)
    pieces = [from_root(first_low, "row", col_id * ratio + offset_q) for offset_q in range(ratio)]
    col_first = jnp.concatenate(pieces, axis=0)
    product1 = jnp.dot(tile, col_first, preferred_element_type=jnp.float32)
    second = refine(first, product1)
    return (first, second)


EDGE = 256
STEP = 128
PAD = 384


def prepare_kernel(*refs):
    count = 6
    sources, (block, side, lent), copies = refs[:count], refs[count : count + 3], refs[count + 3 :]
    done = copies[count]
    moves = []
    for k in range(count):
        move = pltpu.make_async_copy(sources[k], copies[k], done.at[k])
        move.start()
        moves.append(move)
    for move in moves:
        move.wait()
    telemetry, scales, start, target, noise, bands = copies[:count]
    lent[...] = bands[...]
    panel, chunk = start.shape
    slopes = telemetry[...].astype(jnp.float32) * scales[...].astype(jnp.float32) / 128.0
    block[0:panel, :] = start[...]
    block[panel:, :] = slopes.astype(jnp.bfloat16)
    pieces = target.shape[1] // STEP
    for piece in range(pieces):
        part = slice(piece * STEP, (piece + 1) * STEP)
        side[piece * panel : (piece + 1) * panel, :] = target[:, part]
    rest = jnp.concatenate(
        [noise[:, piece * STEP : (piece + 1) * STEP] for piece in range(pieces)], axis=0
    )
    planes = []
    for _ in range(3):
        plane = rest.astype(jnp.bfloat16).astype(jnp.float32)
        rest = rest - plane
        planes.append(plane)
    planes.append(jnp.zeros_like(rest))
    side[pieces * panel :, :] = jnp.concatenate(planes, axis=0).astype(jnp.bfloat16)


def spot(row):
    return row + row // SUBAP * (2 * PAD) + PAD


def column(ref, begin, width, rows=slice(None)):
    return ref[rows, pl.ds(pl.multiple_of(begin, STEP), width)]


def moments(panel_ref, flat, sums):
    panel = 64
    local = (lax.broadcasted_iota(jnp.int32, (panel, STEP), 1) - STEP // 2).astype(jnp.float32)
    for sensor in range(sums.shape[0]):
        plain = jnp.zeros((panel, 128), jnp.float32)
        moved = jnp.zeros((panel, 128), jnp.float32)
        for t in range(SUBAP // STEP):
            sums[sensor, t, 0:panel, :] = plain
            sums[sensor, t, panel:, :] = moved
            begin = sensor * (SUBAP + 2 * PAD) + PAD + t * STEP
            x = panel_ref[0:panel, begin : begin + STEP]
            xq = (x.astype(jnp.float32) * local).astype(jnp.bfloat16)
            both = jnp.dot(
                jnp.concatenate([x, xq], axis=0),
                flat[begin : begin + STEP, :],
                preferred_element_type=jnp.float32,
            )
            plain = plain + both[0:panel]
            moved = moved + (both[panel:] + both[0:panel] * float(t * STEP + STEP // 2))
        sums[sensor, SUBAP // STEP, 0:panel, :] = plain
        sums[sensor, SUBAP // STEP, panel:, :] = moved


def multiply(base, norm_count, bands, panel_ref, wide, flat, sums, lines, accs):
    panel = 64
    scale = 1.0 / norm_count
    sensors = sums.shape[0]
    sensor = base // SUBAP
    count = len(lines)
    rows_i = lax.broadcasted_iota(jnp.int32, (PAD, EDGE), 0)
    cols_i = lax.broadcasted_iota(jnp.int32, (PAD, EDGE), 1)
    ramp = (rows_i - cols_i).astype(jnp.float32)
    square = ramp[0:EDGE]
    eye = rows_i[0:EDGE] == cols_i[0:EDGE]
    local = (lax.broadcasted_iota(jnp.int32, (panel, EDGE), 1) - EDGE // 2).astype(jnp.float32)
    slopes = []
    for k in range(count):
        both = column(wide, spot(base) + k * EDGE, EDGE)
        keep = lax.broadcasted_iota(jnp.int32, both.shape, 0) >= panel
        slopes.append(jnp.where(keep, both, jnp.zeros_like(both)))
    place = [base % SUBAP + k * EDGE for k in range(count)]
    width = [bands[jnp.minimum(sensor, b), jnp.maximum(sensor, b)] for b in range(sensors)]
    low = [[jnp.minimum((p - w) // STEP * STEP, p - PAD) for p in place] for w in width]
    high = [[jnp.maximum((p + w) // STEP * STEP, p + EDGE) for p in place] for w in width]

    def raw_at(k, begin, size):
        return jnp.dot(
            flat[pl.ds(pl.multiple_of(begin, STEP), size), :],
            slopes[k],
            preferred_element_type=jnp.float32,
        )

    def carry(k, begin, size, entry):
        return jnp.dot(
            column(panel_ref, begin, size, slice(0, panel)), entry, preferred_element_type=jnp.float32
        )

    for k in range(count):
        total = jnp.zeros((panel, EDGE), jnp.float32)
        near = jnp.zeros((panel, 128), jnp.float32)
        tilt = jnp.zeros((panel, 128), jnp.float32)
        middle = (place[k] + EDGE // 2).astype(jnp.float32)
        for b in range(sensors):
            rate = 1.0 / jnp.full((panel, 128), width[b].astype(jnp.float32))
            at = [
                jnp.maximum(low[b][k] + PAD, 0) // STEP,
                place[k] // STEP,
                (place[k] + EDGE) // STEP,
                jnp.minimum(high[b][k], SUBAP) // STEP,
            ]
            zero = [sums[b, t, 0:panel, :] for t in at]
            one = [sums[b, t, panel:, :] for t in at]
            left, right = zero[1] - zero[0], zero[3] - zero[2]
            left_q, right_q = one[1] - one[0], one[3] - one[2]
            near += left + right + rate * ((left_q - middle * left) - (right_q - middle * right))
            tilt += rate * (right - left)
            begin = b * (SUBAP + 2 * PAD) + PAD + place[k]
            fall = (1.0 / jnp.full((EDGE, EDGE), width[b].astype(jnp.float32))) * scale
            taper = jnp.maximum(0.0, scale - jnp.abs(square) * fall)
            same = (sensor == b).astype(jnp.float32)
            entry = taper * raw_at(k, begin, EDGE) + jnp.where(eye, lines[k] * same, 0.0)
            total += carry(k, begin, EDGE, entry.astype(jnp.bfloat16))
        mix = jnp.concatenate([near, tilt], axis=0) * scale
        mix_high = mix.astype(jnp.bfloat16)
        mix_low = (mix - mix_high.astype(jnp.float32)).astype(jnp.bfloat16)
        far = jnp.dot(mix_high, slopes[k], preferred_element_type=jnp.float32)
        far += jnp.dot(mix_low, slopes[k], preferred_element_type=jnp.float32)
        accs[k][...] = total + far[0:panel] + local * far[panel:]

    for b in range(sensors):
        for side in (0, 1):
            begins = low[b] if side == 0 else high[b]
            wanted = low[b][count - 1] + PAD > 0 if side == 0 else high[b][0] < SUBAP

            @pl.when(wanted)
            def _(b=b, side=side, begins=begins):
                fall = (1.0 / jnp.full((PAD, EDGE), width[b].astype(jnp.float32))) * scale
                for k in range(count):
                    inside = jnp.maximum(begins[k], -PAD) if side == 0 else jnp.minimum(begins[k], SUBAP)
                    begin = b * (SUBAP + 2 * PAD) + PAD + inside
                    gap = (inside - place[k]).astype(jnp.float32)
                    away = ramp + gap
                    if side == 0:
                        taper = jnp.maximum(0.0, scale + away * fall)
                    else:
                        taper = jnp.maximum(0.0, scale - away * fall)
                    entry = (taper * raw_at(k, begin, PAD)).astype(jnp.bfloat16)
                    accs[k][...] += carry(k, begin, PAD, entry)


def first_kernel(sizes, ids, bands, *refs):
    rows_n, cols_n, chunk, height, panel, norm_count, hops = sizes
    half = rows_n // 2
    mine, other = refs[:half], refs[half : 2 * half]
    wide, flat, low, first, keep, weight, sums, goals, noises, acc = refs[2 * half :]
    count = height // EDGE
    col_id, row_id = ids[0], ids[1]
    core = row_id % 2
    own = row_id // 2
    stride = SUBAP + 2 * PAD
    for sensor in range(sums.shape[0]):
        for begin in (sensor * stride, sensor * stride + PAD + SUBAP):
            wide[:, begin : begin + PAD] = jnp.zeros((2 * panel, PAD), jnp.bfloat16)
            flat[begin : begin + PAD, :] = jnp.zeros((PAD, 2 * panel), jnp.bfloat16)
    starts = [spot((hop ^ col_id) * (rows_n * chunk)) for hop in hops]
    pieces = height // STEP
    tail = cols_n * chunk
    for j in range(half):
        pos = own ^ j
        for source, parity in ((mine[j], core), (other[j], 1 - core)):
            shift = (2 * pos + parity) * chunk
            for slot in range(cols_n):
                place = pl.multiple_of(starts[slot] + shift, STEP)
                part = source[slot * chunk : (slot + 1) * chunk, :]
                wide[:, pl.ds(place, chunk)] = part
                flat[pl.ds(place, chunk), :] = part.T
        for t in range(pieces):
            goals[j, :, t * STEP : (t + 1) * STEP] = mine[j][tail + t * panel : tail + (t + 1) * panel, :]
        planes = mine[j][tail + pieces * panel : tail + pieces * panel + 16, :].astype(jnp.float32)
        lines = planes[0:pieces] + planes[pieces : 2 * pieces] + planes[2 * pieces : 3 * pieces]
        noises[j, 0:1, :] = jnp.concatenate([lines[t : t + 1] for t in range(pieces)], axis=1)
    moments(wide, flat, sums)
    parts = [slice(k * EDGE, (k + 1) * EDGE) for k in range(count)]

    def block(step, _):
        j = half - 1 - step
        base = (2 * (own ^ j) + core) * height
        lines = [noises[j, 0:1, part] for part in parts]
        accs = [acc.at[k] for k in range(count)]
        multiply(base, norm_count, bands, wide, wide, flat, sums, lines, accs)
        for k, part in enumerate(parts):
            both = column(wide, spot(base) + k * EDGE, EDGE).astype(jnp.float32)
            power = jnp.sum(both[panel:] * both[panel:], axis=0, keepdims=True)
            wgt = damping / (power / norm_count + lines[k])
            goal = goals[j, :, part].astype(jnp.float32)
            new = both[0:panel] + wgt * (goal - acc[k])
            first[:, part] = new
            keep[:, part] = new
            weight[:, part] = jnp.broadcast_to(wgt, (8, EDGE))
            into = pl.multiple_of((own ^ j) * height + k * EDGE, EDGE)
            low[:, pl.ds(into, EDGE)] = new.astype(jnp.bfloat16)
        return 0

    lax.fori_loop(0, half, block, 0)


def second_kernel(sizes, ids, bands, wide, flat, home, away, first, weight, target, noise, second, new, sums, acc):
    rows_n, cols_n, chunk, height, panel, norm_count, hops = sizes
    core = ids[1] % 2
    stride = SUBAP + 2 * PAD
    for sensor in range(sums.shape[0]):
        for begin in (sensor * stride, sensor * stride + PAD + SUBAP):
            new[:, begin : begin + PAD] = jnp.zeros((panel, PAD), jnp.bfloat16)
    for pos in range(rows_n // 2):
        for source, parity in ((home, core), (away, 1 - core)):
            place = pl.multiple_of(spot((2 * pos + parity) * height), STEP)
            new[:, pl.ds(place, height)] = source[:, pos * height : (pos + 1) * height]
    moments(new, flat, sums)
    parts = [slice(k * EDGE, (k + 1) * EDGE) for k in range(height // EDGE)]
    lines = [noise[:, part] for part in parts]
    accs = [acc.at[k] for k in range(height // EDGE)]
    multiply(ids[1] * height, norm_count, bands, new, wide, flat, sums, lines, accs)
    for k, part in enumerate(parts):
        goal = target[:, part].astype(jnp.float32)
        second[:, part] = first[:, part] + weight[0:1, part] * (goal - acc[k])


def flip(block, axis, bit):
    size = lax.axis_size(axis)
    return lax.ppermute(block, axis, [(i, i ^ bit) for i in range(size)])


def gathered_plan(telemetry, scales, bands, noise, start, target):
    rows_n = lax.axis_size("row")
    cols_n = lax.axis_size("col")
    chunk, frames = telemetry.shape
    height, panel = target.shape
    order = chunk * rows_n * cols_n
    sensors = order // SUBAP
    padded = order + 2 * PAD * sensors
    half = rows_n // 2
    ids = jnp.stack([lax.axis_index("col"), lax.axis_index("row")]).astype(jnp.int32)
    vmem = pl.BlockSpec(memory_space=pltpu.VMEM)
    smem = pl.BlockSpec(memory_space=pltpu.SMEM)
    params = pltpu.CompilerParams(vmem_limit_bytes=24 * 1024 * 1024)
    noise = noise.reshape(1, height)
    target = target.T
    own = (telemetry.T, scales.reshape(1, chunk), start.T, target, noise, bands)
    block, side, bands = pl.pallas_call(
        prepare_kernel,
        out_shape=(
            jax.ShapeDtypeStruct((2 * panel, chunk), jnp.bfloat16),
            jax.ShapeDtypeStruct((height // STEP * panel + 16, 128), jnp.bfloat16),
            jax.ShapeDtypeStruct(bands.shape, bands.dtype),
        ),
        in_specs=[pl.BlockSpec(memory_space=pltpu.HBM)] * len(own),
        out_specs=(vmem,) * 3,
        scratch_shapes=[pltpu.VMEM(x.shape, x.dtype) for x in own]
        + [pltpu.SemaphoreType.DMA((len(own),))],
        compiler_params=params,
        name="prepare",
    )(*[pltpu.with_memory_space_constraint(x, pltpu.HBM) for x in own])
    hops = (0,)
    bit = cols_n // 2
    while bit:
        block = jnp.concatenate([block, flip(block, "col", bit)], axis=0)
        hops = hops + tuple(hop ^ bit for hop in hops)
        bit //= 2
    sizes = (rows_n, cols_n, chunk, height, panel, float(order // 4), hops)
    payload = jnp.concatenate([block, side], axis=0)
    mine = [payload] + [flip(payload, "row", 2 * j) for j in range(1, half)]
    other = [flip(part, "row", 1) for part in mine]
    acc = pltpu.VMEM((height // EDGE, panel, EDGE), jnp.float32)
    sums = pltpu.VMEM((sensors, SUBAP // STEP + 1, 2 * panel, 128), jnp.float32)
    wide, flat, low, first, keep, weight = pl.pallas_call(
        functools.partial(first_kernel, sizes),
        out_shape=(
            jax.ShapeDtypeStruct((2 * panel, padded), jnp.bfloat16),
            jax.ShapeDtypeStruct((padded, 2 * panel), jnp.bfloat16),
            jax.ShapeDtypeStruct((panel, half * height), jnp.bfloat16),
            jax.ShapeDtypeStruct((panel, height), jnp.float32),
            jax.ShapeDtypeStruct((panel, height), jnp.float32),
            jax.ShapeDtypeStruct((8, height), jnp.float32),
        ),
        in_specs=[smem, smem] + [vmem] * rows_n,
        out_specs=(vmem,) * 6,
        scratch_shapes=[
            sums,
            pltpu.VMEM((half, panel, height), jnp.bfloat16),
            pltpu.VMEM((half, 8, height), jnp.float32),
            acc,
        ],
        compiler_params=params,
        name="first_pass",
    )(ids, bands, *mine, *other)
    away = flip(low, "row", 1)
    second = pl.pallas_call(
        functools.partial(second_kernel, sizes),
        out_shape=jax.ShapeDtypeStruct((panel, height), jnp.float32),
        in_specs=[smem, smem] + [vmem] * 8,
        out_specs=vmem,
        scratch_shapes=[pltpu.VMEM((panel, padded), jnp.bfloat16), sums, acc],
        compiler_params=params,
        name="second_pass",
    )(ids, bands, wide, flat, low, away, keep, weight, target, noise)
    return (first.T, second.T)


def power_of_two(number):
    return number > 0 and number & (number - 1) == 0


def fits(mesh, telemetry, target):
    rows_n, cols_n = mesh.shape["row"], mesh.shape["col"]
    order, frames = telemetry.shape
    panel = target.shape[1]
    height = order // rows_n
    return (
        power_of_two(rows_n)
        and power_of_two(cols_n)
        and rows_n >= 2
        and frames == panel == 64
        and order % SUBAP == 0
        and SUBAP % height == 0
        and height == 2 * EDGE
        and order // (rows_n * cols_n) == STEP
        and order <= 2 * SUBAP
    )


def solution(mesh):
    def program(telemetry, scales, bands, noise, start, target):
        plan = gathered_plan if fits(mesh, telemetry, target) else tiled_plan
        return jax.shard_map(
            plan,
            mesh=mesh,
            in_specs=(
                P(("col", "row"), None),
                P(("col", "row")),
                P(),
                P("row"),
                P(("col", "row"), None),
                P("row", None),
            ),
            out_specs=(P("row", None), P("row", None)),
            check_vma=False,
        )(telemetry, scales, bands, noise, start, target)

    return program
```

```python
import functools
import math

import jax
import jax.numpy as jnp
from jax import lax
from jax.experimental import pallas as pl
from jax.experimental.pallas import tpu as pltpu
from jax.sharding import PartitionSpec as P

SUBAP = 2048


damping = 0.4


def from_root(block, axis, holder):
    block = jnp.where(lax.axis_index(axis) == holder, block, jnp.zeros_like(block))
    return lax.psum(block, axis)


def tiled_plan(telemetry, scales, bands, noise, start, target):
    frame_count = telemetry.shape[1]
    row_count = lax.axis_size("row")
    col_count = lax.axis_size("col")
    ratio = row_count // col_count
    row_id = lax.axis_index("row")
    col_id = lax.axis_index("col")
    order_total = telemetry.shape[0] * row_count * col_count
    norm_count = jnp.float32(order_total // 4)
    slopes = (telemetry.astype(jnp.float32) * scales.astype(jnp.float32)[:, None] / 128.0).astype(
        jnp.bfloat16
    )
    joined = jnp.concatenate([slopes, start], axis=1)
    col_joined = lax.all_gather(joined, "row", axis=0, tiled=True)
    col_width = col_joined.shape[0]
    row_height = col_width // ratio
    half = lax.dynamic_slice_in_dim(col_joined, row_id % ratio * row_height, row_height, 0)
    row_joined = from_root(half, "col", row_id // ratio)
    row_slopes = row_joined[:, :frame_count]
    row_start = row_joined[:, frame_count:]
    col_slopes = col_joined[:, :frame_count]
    col_start = col_joined[:, frame_count:]
    panel_width = col_start.shape[1]
    row_f = row_slopes.astype(jnp.float32)
    weight = damping / (jnp.sum(row_f * row_f, axis=1) / norm_count + noise)
    count = bands.shape[0]
    index = jnp.arange(count, dtype=jnp.int32)
    sym = jnp.where(index[:, None] <= index[None, :], bands, bands.T).astype(jnp.float32)
    row_ids = row_id * row_height + jnp.arange(row_height, dtype=jnp.int32)
    onehot = (row_ids[:, None] // SUBAP == index[None, :]).astype(jnp.float32)
    row_band = jnp.dot(onehot, sym, precision=lax.Precision.HIGHEST)
    row_pos = (row_ids % SUBAP).astype(jnp.float32)
    width = math.gcd(math.gcd(col_width, 512), SUBAP)
    nblocks = col_width // width

    def build(step, carry):
        tile, acc = carry
        offset = step * width
        cols = lax.dynamic_slice_in_dim(col_slopes, offset, width, 0)
        raw = (
            lax.dot_general(
                row_slopes, cols, (((1,), (1,)), ((), ())), preferred_element_type=jnp.float32
            )
            / norm_count
        )
        col_ids = col_id * col_width + offset + jnp.arange(width, dtype=jnp.int32)
        band = lax.dynamic_slice_in_dim(row_band, (col_id * col_width + offset) // SUBAP, 1, 1)
        dist = jnp.abs(row_pos[:, None] - (col_ids % SUBAP).astype(jnp.float32)[None, :])
        taper = jnp.maximum(0.0, 1.0 - dist / band)
        diag = jnp.where(row_ids[:, None] == col_ids[None, :], noise[:, None], jnp.float32(0.0))
        entry = (taper * raw + diag).astype(jnp.bfloat16)
        tile = lax.dynamic_update_slice_in_dim(tile, entry, offset, 1)
        return (tile, acc)

    tile_init = jnp.zeros((row_height, col_width), jnp.bfloat16)
    acc_init = jnp.zeros((row_height, panel_width), jnp.float32)
    tile, acc = lax.fori_loop(0, nblocks, build, (tile_init, acc_init))
    product0 = jnp.dot(tile, col_start, preferred_element_type=jnp.float32)
    target_f = target.astype(jnp.float32)

    def refine(current, product):
        share = lax.psum_scatter(product, "col", scatter_dimension=0, tiled=True)
        share_rows = row_height // col_count
        begin = col_id * share_rows
        cur_part = lax.dynamic_slice_in_dim(current, begin, share_rows, 0)
        tgt_part = lax.dynamic_slice_in_dim(target_f, begin, share_rows, 0)
        wgt_part = lax.dynamic_slice_in_dim(weight, begin, share_rows, 0)
        updated = cur_part + wgt_part[:, None] * (tgt_part - share)
        return lax.all_gather(updated, "col", axis=0, tiled=True)

    first = refine(row_start.astype(jnp.float32), product0)
    first_low = first.astype(jnp.bfloat16)
    pieces = [from_root(first_low, "row", col_id * ratio + offset_q) for offset_q in range(ratio)]
    col_first = jnp.concatenate(pieces, axis=0)
    product1 = jnp.dot(tile, col_first, preferred_element_type=jnp.float32)
    second = refine(first, product1)
    return (first, second)


EDGE = 256
STEP = 128
PAD = 384
ROUND = 4


def prepare_kernel(*refs):
    count = 6
    sources, (block, side, lent), copies = refs[:count], refs[count : count + 3], refs[count + 3 :]
    done = copies[count]
    moves = []
    for k in range(count):
        move = pltpu.make_async_copy(sources[k], copies[k], done.at[k])
        move.start()
        moves.append(move)
    for move in moves:
        move.wait()
    telemetry, scales, start, target, noise, bands = copies[:count]
    lent[...] = bands[...]
    panel, chunk = start.shape
    slopes = telemetry[...].astype(jnp.float32) * scales[...].astype(jnp.float32) / 128.0
    block[0:panel, :] = start[...]
    block[panel:, :] = slopes.astype(jnp.bfloat16)
    pieces = target.shape[1] // STEP
    for piece in range(pieces):
        part = slice(piece * STEP, (piece + 1) * STEP)
        side[piece * panel : (piece + 1) * panel, :] = target[:, part]
    rest = jnp.concatenate(
        [noise[:, piece * STEP : (piece + 1) * STEP] for piece in range(pieces)], axis=0
    )
    planes = []
    for _ in range(3):
        plane = rest.astype(jnp.bfloat16).astype(jnp.float32)
        rest = rest - plane
        planes.append(plane)
    planes.append(jnp.zeros_like(rest))
    side[pieces * panel :, :] = jnp.concatenate(planes, axis=0).astype(jnp.bfloat16)


def spot(row):
    return row + row // SUBAP * (2 * PAD) + PAD


def column(ref, begin, width, rows=slice(None)):
    return ref[rows, pl.ds(pl.multiple_of(begin, STEP), width)]


def moments(panel_ref, flat, sums):
    panel = 64
    local = (lax.broadcasted_iota(jnp.int32, (panel, STEP), 1) - STEP // 2).astype(jnp.float32)
    for sensor in range(sums.shape[0]):
        begins = [padded_start(sensor) + t * STEP for t in range(SUBAP // STEP)]
        dots = []
        for begin in begins:
            x = panel_ref[0:panel, begin : begin + STEP]
            xq = (x.astype(jnp.float32) * local).astype(jnp.bfloat16)
            dots.append(
                jnp.dot(
                    jnp.concatenate([x, xq], axis=0),
                    flat[begin : begin + STEP, :],
                    preferred_element_type=jnp.float32,
                )
            )
        plain = jnp.zeros((panel, 128), jnp.float32)
        moved = jnp.zeros((panel, 128), jnp.float32)
        for t, both in enumerate(dots):
            sums[sensor, t, 0:panel, :] = plain
            sums[sensor, t, panel:, :] = moved
            plain = plain + both[0:panel]
            moved = moved + (both[panel:] + both[0:panel] * float(t * STEP + STEP // 2))
        sums[sensor, SUBAP // STEP, 0:panel, :] = plain
        sums[sensor, SUBAP // STEP, panel:, :] = moved


def fill_ramp(ramp):
    rows = lax.broadcasted_iota(jnp.int32, ramp.shape, 0)
    cols = lax.broadcasted_iota(jnp.int32, ramp.shape, 1)
    ramp[...] = (rows - cols).astype(jnp.float32)


def padded_start(sensor):
    return sensor * (SUBAP + 2 * PAD) + PAD


def clear_pads(ref, axis, sensors):
    for sensor in range(sensors):
        for begin in (padded_start(sensor) - PAD, padded_start(sensor) + SUBAP):
            if axis:
                ref[:, begin : begin + PAD] = jnp.zeros((ref.shape[0], PAD), ref.dtype)
            else:
                ref[begin : begin + PAD, :] = jnp.zeros((PAD, ref.shape[1]), ref.dtype)


def keep_slopes(wide, base, height, own_slopes, at):
    panel = wide.shape[0] // 2
    own_slopes[0:panel, at : at + height] = jnp.zeros((panel, height), own_slopes.dtype)
    own_slopes[panel:, at : at + height] = column(wide, spot(base), height, slice(panel, None))


def edges(place, width):
    low = jnp.minimum((place - width) & -STEP, place - PAD)
    high = jnp.maximum((place + width) & -STEP, place + EDGE)
    return low, high


def widths(bands, sensor, sensors):
    return [bands[jnp.minimum(sensor, b), jnp.maximum(sensor, b)] for b in range(sensors)]


def list_jobs(bands, bases, height, sensors, jobs):
    number = jnp.int32(0)
    for group, base in enumerate(bases):
        sensor = base // SUBAP
        for b, width in enumerate(widths(bands, sensor, sensors)):
            for k in range(height // EDGE):
                place = base - sensor * SUBAP + k * EDGE
                low, high = edges(place, width)
                for begin, wanted in ((low, low + PAD > 0), (high, high < SUBAP)):
                    jobs[0, number] = group * (height // EDGE) + k
                    jobs[1, number] = begin + padded_start(b)
                    jobs[2, number] = begin - place
                    jobs[3, number] = width
                    number = number + wanted.astype(jnp.int32)
    for fill in range(ROUND - 1):
        for field, value in enumerate((0, 0, 0, 1)):
            jobs[field, number + fill] = value
    return (number + (ROUND - 1)) // ROUND


def near_and_far(base, group, norm_count, bands, panel_ref, flat, own_slopes, sums, ramp, noise, acc):
    panel = acc.shape[1]
    scale = 1.0 / norm_count
    sensors = sums.shape[0]
    sensor = base // SUBAP
    count = noise.shape[1] // EDGE
    local = (lax.broadcasted_iota(jnp.int32, (1, EDGE), 1) - EDGE // 2).astype(jnp.float32)
    width = widths(bands, sensor, sensors)
    rates = [1.0 / jnp.full((1, EDGE), w.astype(jnp.float32)) for w in width]
    places = [base - sensor * SUBAP + k * EDGE for k in range(count)]
    slopes = [column(own_slopes, (group * count + k) * EDGE, EDGE) for k in range(count)]
    begins = [[pl.multiple_of(padded_start(b) + p, STEP) for b in range(sensors)] for p in places]
    raws = [
        jnp.dot(
            jnp.concatenate([flat[pl.ds(begin, EDGE), :] for begin in begins[k]], axis=0),
            slopes[k],
            preferred_element_type=jnp.float32,
        )
        for k in range(count)
    ]
    fars = []
    for k in range(count):
        near = jnp.zeros((panel, 128), jnp.float32)
        tilt = jnp.zeros((panel, 128), jnp.float32)
        middle = (places[k] + EDGE // 2).astype(jnp.float32)
        for b in range(sensors):
            low, high = edges(places[k], width[b])
            rate = rates[b][:, 0:128]
            at = [
                jnp.maximum(low + PAD, 0) // STEP,
                places[k] // STEP,
                (places[k] + EDGE) // STEP,
                jnp.minimum(high, SUBAP) // STEP,
            ]
            zero = [sums[b, t, 0:panel, :] for t in at]
            one = [sums[b, t, panel:, :] for t in at]
            left, right = zero[1] - zero[0], zero[3] - zero[2]
            left_q, right_q = one[1] - one[0], one[3] - one[2]
            near += left + right + rate * ((left_q - middle * left) - (right_q - middle * right))
            tilt += rate * (right - left)
        mix = jnp.concatenate([near, tilt], axis=0) * scale
        mix_high = mix.astype(jnp.bfloat16)
        mix_low = (mix - mix_high.astype(jnp.float32)).astype(jnp.bfloat16)
        far = jnp.dot(
            jnp.concatenate([mix_high, mix_low], axis=0), slopes[k], preferred_element_type=jnp.float32
        )
        fars.append(far[0 : 2 * panel] + far[2 * panel :])
    square = ramp[0:EDGE, :]
    entries = []
    for k in range(count):
        line = noise[:, k * EDGE : (k + 1) * EDGE]
        for b in range(sensors):
            taper = jnp.maximum(0.0, scale - jnp.abs(square) * (rates[b] * scale))
            same = (sensor == b).astype(jnp.float32)
            entry = taper * raws[k][b * EDGE : (b + 1) * EDGE]
            entry = entry + jnp.where(square == 0.0, line * same, 0.0)
            entries.append(entry.astype(jnp.bfloat16))
    for k in range(count):
        total = fars[k][0:panel] + local * fars[k][panel:]
        for b in range(sensors):
            total += jnp.dot(
                column(panel_ref, begins[k][b], EDGE, slice(0, panel)),
                entries[k * sensors + b],
                preferred_element_type=jnp.float32,
            )
        acc[group * count + k] = total


def run_jobs(rounds, norm_count, panel_ref, flat, own_slopes, ramp, jobs, acc):
    panel = acc.shape[1]
    scale = 1.0 / norm_count

    def body(step, _):
        picked = [[jobs[field, step * ROUND + u] for field in range(4)] for u in range(ROUND)]
        begins = [pl.multiple_of(job[1], STEP) for job in picked]
        raws = [
            jnp.dot(
                flat[pl.ds(begin, PAD), :],
                column(own_slopes, job[0] * EDGE, EDGE),
                preferred_element_type=jnp.float32,
            )
            for job, begin in zip(picked, begins)
        ]
        entries = []
        for (tile, begin, gap, width), raw in zip(picked, raws):
            fall = scale / jnp.full((1, EDGE), width.astype(jnp.float32))
            taper = jnp.maximum(0.0, scale - jnp.abs(ramp[...] + gap.astype(jnp.float32)) * fall)
            entries.append((taper * raw).astype(jnp.bfloat16))
        parts = [
            jnp.dot(
                column(panel_ref, begin, PAD, slice(0, panel)), entry, preferred_element_type=jnp.float32
            )
            for begin, entry in zip(begins, entries)
        ]
        for job, part in zip(picked, parts):
            acc[job[0]] += part
        return 0

    lax.fori_loop(0, rounds, body, 0)


def first_kernel(sizes, ids, bands_in, *refs):
    rows_n, cols_n, chunk, height, panel, norm_count, hops = sizes
    half = rows_n // 2
    mine, other = refs[:half], refs[half : 2 * half]
    wide, flat, low, first, weight = refs[2 * half : 2 * half + 5]
    sums, noises, acc, ramp, own_slopes, bands, jobs, done = refs[2 * half + 5 :]
    lend = pltpu.make_async_copy(bands_in, bands, done)
    lend.start()
    sensors = sums.shape[0]
    col_id, row_id = ids[0], ids[1]
    core = row_id % 2
    own = row_id // 2
    clear_pads(wide, 1, sensors)
    clear_pads(flat, 0, sensors)
    starts = [spot((hop ^ col_id) * (rows_n * chunk)) for hop in hops]
    pieces = height // STEP
    tail = cols_n * chunk
    for j in range(half):
        pos = own ^ j
        for source, parity in ((mine[j], core), (other[j], 1 - core)):
            shift = (2 * pos + parity) * chunk
            for slot in range(cols_n):
                place = pl.multiple_of(starts[slot] + shift, STEP)
                part = source[slot * chunk : (slot + 1) * chunk, :]
                wide[:, pl.ds(place, chunk)] = part
                flat[pl.ds(place, chunk), :] = part.T
        planes = mine[j][tail + pieces * panel : tail + pieces * panel + 16, :].astype(jnp.float32)
        lines = planes[0:pieces] + planes[pieces : 2 * pieces] + planes[2 * pieces : 3 * pieces]
        noises[j, 0:1, :] = jnp.concatenate([lines[t : t + 1] for t in range(pieces)], axis=1)
    moments(wide, flat, sums)
    fill_ramp(ramp)
    bases = [(2 * (own ^ j) + core) * height for j in range(half)]
    for j in range(half):
        keep_slopes(wide, bases[j], height, own_slopes, j * height)
    lend.wait()
    rounds = list_jobs(bands, bases, height, sensors, jobs)

    def block(j, _):
        base = (2 * (own ^ j) + core) * height
        noise = noises[j, 0:1, :]
        near_and_far(base, j, norm_count, bands, wide, flat, own_slopes, sums, ramp, noise, acc)
        return 0

    lax.fori_loop(0, half, block, 0)
    run_jobs(rounds, norm_count, wide, flat, own_slopes, ramp, jobs, acc)
    for j in range(half):
        for k in range(height // EDGE):
            part = slice(k * EDGE, (k + 1) * EDGE)
            both = column(wide, spot(bases[j]) + k * EDGE, EDGE).astype(jnp.float32)
            power = jnp.sum(both[panel:] * both[panel:], axis=0, keepdims=True)
            wgt = damping / (power / norm_count + noises[j, 0:1, part])
            goal = jnp.concatenate(
                [
                    mine[j][tail + t * panel : tail + (t + 1) * panel, :]
                    for t in range(k * EDGE // STEP, (k + 1) * EDGE // STEP)
                ],
                axis=1,
            ).astype(jnp.float32)
            new = both[0:panel] + wgt * (goal - acc[j * (height // EDGE) + k])
            if j == 0:
                first[:, part] = new
                weight[:, part] = jnp.broadcast_to(wgt, (8, EDGE))
            into = pl.multiple_of((own ^ j) * height + k * EDGE, EDGE)
            low[:, pl.ds(into, EDGE)] = new.astype(jnp.bfloat16)


def second_kernel(sizes, ids, bands_in, wide, flat, home, away, first, weight, target, noise, *refs):
    second, first_out, new, sums, acc, ramp, own_slopes, bands, jobs, done = refs
    rows_n, cols_n, chunk, height, panel, norm_count, hops = sizes
    lend = pltpu.make_async_copy(bands_in, bands, done.at[0])
    lend.start()
    give = pltpu.make_async_copy(first, first_out, done.at[1])
    give.start()
    sensors = sums.shape[0]
    core = ids[1] % 2
    clear_pads(new, 1, sensors)
    for pos in range(rows_n // 2):
        for source, parity in ((home, core), (away, 1 - core)):
            place = pl.multiple_of(spot((2 * pos + parity) * height), STEP)
            new[:, pl.ds(place, height)] = source[:, pos * height : (pos + 1) * height]
    moments(new, flat, sums)
    fill_ramp(ramp)
    base = ids[1] * height
    keep_slopes(wide, base, height, own_slopes, 0)
    lend.wait()
    rounds = list_jobs(bands, [base], height, sensors, jobs)
    near_and_far(base, 0, norm_count, bands, new, flat, own_slopes, sums, ramp, noise[...], acc)
    run_jobs(rounds, norm_count, new, flat, own_slopes, ramp, jobs, acc)
    for k in range(height // EDGE):
        part = slice(k * EDGE, (k + 1) * EDGE)
        goal = target[:, part].astype(jnp.float32)
        second[:, part] = first[:, part] + weight[0:1, part] * (goal - acc[k])
    give.wait()


def flip(block, axis, bit):
    size = lax.axis_size(axis)
    return lax.ppermute(block, axis, [(i, i ^ bit) for i in range(size)])


def gathered_plan(telemetry, scales, bands, noise, start, target):
    rows_n = lax.axis_size("row")
    cols_n = lax.axis_size("col")
    chunk, frames = telemetry.shape
    height, panel = target.shape
    order = chunk * rows_n * cols_n
    sensors = order // SUBAP
    padded = order + 2 * PAD * sensors
    half = rows_n // 2
    ids = jnp.stack([lax.axis_index("col"), lax.axis_index("row")]).astype(jnp.int32)
    vmem = pl.BlockSpec(memory_space=pltpu.VMEM)
    smem = pl.BlockSpec(memory_space=pltpu.SMEM)
    params = pltpu.CompilerParams(vmem_limit_bytes=24 * 1024 * 1024)
    noise = noise.reshape(1, height)
    target = target.T
    own = (telemetry.T, scales.reshape(1, chunk), start.T, target, noise, bands)
    block, side, bands = pl.pallas_call(
        prepare_kernel,
        out_shape=(
            jax.ShapeDtypeStruct((2 * panel, chunk), jnp.bfloat16),
            jax.ShapeDtypeStruct((height // STEP * panel + 16, 128), jnp.bfloat16),
            jax.ShapeDtypeStruct(bands.shape, bands.dtype),
        ),
        in_specs=[pl.BlockSpec(memory_space=pltpu.HBM)] * len(own),
        out_specs=(vmem,) * 3,
        scratch_shapes=[pltpu.VMEM(x.shape, x.dtype) for x in own]
        + [pltpu.SemaphoreType.DMA((len(own),))],
        compiler_params=params,
        name="prepare",
    )(*[pltpu.with_memory_space_constraint(x, pltpu.HBM) for x in own])
    hops = (0,)
    bit = cols_n // 2
    while bit:
        block = jnp.concatenate([block, flip(block, "col", bit)], axis=0)
        hops = hops + tuple(hop ^ bit for hop in hops)
        bit //= 2
    sizes = (rows_n, cols_n, chunk, height, panel, float(order // 4), hops)
    payload = jnp.concatenate([block, side], axis=0)
    mine = [payload] + [flip(payload, "row", 2 * j) for j in range(1, half)]
    other = [flip(part, "row", 1) for part in mine]
    tiles = height // EDGE
    sums = pltpu.VMEM((sensors, SUBAP // STEP + 1, 2 * panel, 128), jnp.float32)
    ramp = pltpu.VMEM((PAD, EDGE), jnp.float32)
    lent = pltpu.SMEM(bands.shape, bands.dtype)

    def scratch(groups):
        return [
            pltpu.VMEM((groups * tiles, panel, EDGE), jnp.float32),
            ramp,
            pltpu.VMEM((2 * panel, groups * height), jnp.bfloat16),
            lent,
            pltpu.SMEM((4, groups * tiles * sensors * 2 + ROUND), jnp.int32),
        ]

    wide, flat, low, first, weight = pl.pallas_call(
        functools.partial(first_kernel, sizes),
        out_shape=(
            jax.ShapeDtypeStruct((2 * panel, padded), jnp.bfloat16),
            jax.ShapeDtypeStruct((padded, 2 * panel), jnp.bfloat16),
            jax.ShapeDtypeStruct((panel, half * height), jnp.bfloat16),
            jax.ShapeDtypeStruct((panel, height), jnp.float32),
            jax.ShapeDtypeStruct((8, height), jnp.float32),
        ),
        in_specs=[smem] + [vmem] * (1 + rows_n),
        out_specs=(vmem,) * 5,
        scratch_shapes=[sums, pltpu.VMEM((half, 8, height), jnp.float32)]
        + scratch(half)
        + [pltpu.SemaphoreType.DMA],
        compiler_params=params,
        name="first_pass",
    )(ids, bands, *mine, *other)
    away = flip(low, "row", 1)
    second, first = pl.pallas_call(
        functools.partial(second_kernel, sizes),
        out_shape=(jax.ShapeDtypeStruct((panel, height), jnp.float32),) * 2,
        in_specs=[smem] + [vmem] * 9,
        out_specs=(vmem, pl.BlockSpec(memory_space=pl.ANY)),
        scratch_shapes=[pltpu.VMEM((panel, padded), jnp.bfloat16), sums]
        + scratch(1)
        + [pltpu.SemaphoreType.DMA((2,))],
        compiler_params=params,
        name="second_pass",
    )(ids, bands, wide, flat, low, away, first, weight, target, noise)
    return (first.T, second.T)


def power_of_two(number):
    return number > 0 and number & (number - 1) == 0


def fits(mesh, telemetry, target):
    rows_n, cols_n = mesh.shape["row"], mesh.shape["col"]
    order, frames = telemetry.shape
    panel = target.shape[1]
    height = order // rows_n
    return (
        power_of_two(rows_n)
        and power_of_two(cols_n)
        and rows_n >= 2
        and frames == panel == 64
        and order % SUBAP == 0
        and SUBAP % height == 0
        and height == 2 * EDGE
        and order // (rows_n * cols_n) == STEP
        and order <= 2 * SUBAP
    )


def solution(mesh):
    def program(telemetry, scales, bands, noise, start, target):
        plan = gathered_plan if fits(mesh, telemetry, target) else tiled_plan
        return jax.shard_map(
            plan,
            mesh=mesh,
            in_specs=(
                P(("col", "row"), None),
                P(("col", "row")),
                P(),
                P("row"),
                P(("col", "row"), None),
                P("row", None),
            ),
            out_specs=(P("row", None), P("row", None)),
            check_vma=False,
        )(telemetry, scales, bands, noise, start, target)

    return program
```

```python
import functools
import math

import jax
import jax.numpy as jnp
from jax import lax
from jax.experimental import pallas as pl
from jax.experimental.pallas import tpu as pltpu
from jax.sharding import PartitionSpec as P

SUBAP = 2048


damping = 0.4


def from_root(block, axis, holder):
    block = jnp.where(lax.axis_index(axis) == holder, block, jnp.zeros_like(block))
    return lax.psum(block, axis)


def tiled_plan(telemetry, scales, bands, noise, start, target):
    frame_count = telemetry.shape[1]
    row_count = lax.axis_size("row")
    col_count = lax.axis_size("col")
    ratio = row_count // col_count
    row_id = lax.axis_index("row")
    col_id = lax.axis_index("col")
    order_total = telemetry.shape[0] * row_count * col_count
    norm_count = jnp.float32(order_total // 4)
    slopes = (telemetry.astype(jnp.float32) * scales.astype(jnp.float32)[:, None] / 128.0).astype(
        jnp.bfloat16
    )
    joined = jnp.concatenate([slopes, start], axis=1)
    col_joined = lax.all_gather(joined, "row", axis=0, tiled=True)
    col_width = col_joined.shape[0]
    row_height = col_width // ratio
    half = lax.dynamic_slice_in_dim(col_joined, row_id % ratio * row_height, row_height, 0)
    row_joined = from_root(half, "col", row_id // ratio)
    row_slopes = row_joined[:, :frame_count]
    row_start = row_joined[:, frame_count:]
    col_slopes = col_joined[:, :frame_count]
    col_start = col_joined[:, frame_count:]
    panel_width = col_start.shape[1]
    row_f = row_slopes.astype(jnp.float32)
    weight = damping / (jnp.sum(row_f * row_f, axis=1) / norm_count + noise)
    count = bands.shape[0]
    index = jnp.arange(count, dtype=jnp.int32)
    sym = jnp.where(index[:, None] <= index[None, :], bands, bands.T).astype(jnp.float32)
    row_ids = row_id * row_height + jnp.arange(row_height, dtype=jnp.int32)
    onehot = (row_ids[:, None] // SUBAP == index[None, :]).astype(jnp.float32)
    row_band = jnp.dot(onehot, sym, precision=lax.Precision.HIGHEST)
    row_pos = (row_ids % SUBAP).astype(jnp.float32)
    width = math.gcd(math.gcd(col_width, 512), SUBAP)
    nblocks = col_width // width

    def build(step, carry):
        tile, acc = carry
        offset = step * width
        cols = lax.dynamic_slice_in_dim(col_slopes, offset, width, 0)
        raw = (
            lax.dot_general(
                row_slopes, cols, (((1,), (1,)), ((), ())), preferred_element_type=jnp.float32
            )
            / norm_count
        )
        col_ids = col_id * col_width + offset + jnp.arange(width, dtype=jnp.int32)
        band = lax.dynamic_slice_in_dim(row_band, (col_id * col_width + offset) // SUBAP, 1, 1)
        dist = jnp.abs(row_pos[:, None] - (col_ids % SUBAP).astype(jnp.float32)[None, :])
        taper = jnp.maximum(0.0, 1.0 - dist / band)
        diag = jnp.where(row_ids[:, None] == col_ids[None, :], noise[:, None], jnp.float32(0.0))
        entry = (taper * raw + diag).astype(jnp.bfloat16)
        tile = lax.dynamic_update_slice_in_dim(tile, entry, offset, 1)
        return (tile, acc)

    tile_init = jnp.zeros((row_height, col_width), jnp.bfloat16)
    acc_init = jnp.zeros((row_height, panel_width), jnp.float32)
    tile, acc = lax.fori_loop(0, nblocks, build, (tile_init, acc_init))
    product0 = jnp.dot(tile, col_start, preferred_element_type=jnp.float32)
    target_f = target.astype(jnp.float32)

    def refine(current, product):
        share = lax.psum_scatter(product, "col", scatter_dimension=0, tiled=True)
        share_rows = row_height // col_count
        begin = col_id * share_rows
        cur_part = lax.dynamic_slice_in_dim(current, begin, share_rows, 0)
        tgt_part = lax.dynamic_slice_in_dim(target_f, begin, share_rows, 0)
        wgt_part = lax.dynamic_slice_in_dim(weight, begin, share_rows, 0)
        updated = cur_part + wgt_part[:, None] * (tgt_part - share)
        return lax.all_gather(updated, "col", axis=0, tiled=True)

    first = refine(row_start.astype(jnp.float32), product0)
    first_low = first.astype(jnp.bfloat16)
    pieces = [from_root(first_low, "row", col_id * ratio + offset_q) for offset_q in range(ratio)]
    col_first = jnp.concatenate(pieces, axis=0)
    product1 = jnp.dot(tile, col_first, preferred_element_type=jnp.float32)
    second = refine(first, product1)
    return (first, second)


EDGE = 256
STEP = 128
PAD = 384
ROUND = 4


def prepare_kernel(*refs):
    count = 6
    sources, (block, side, lent), copies = refs[:count], refs[count : count + 3], refs[count + 3 :]
    done = copies[count]
    moves = []
    for k in range(count):
        move = pltpu.make_async_copy(sources[k], copies[k], done.at[k])
        move.start()
        moves.append(move)
    for move in moves:
        move.wait()
    telemetry, scales, start, target, noise, bands = copies[:count]
    lent[...] = bands[...]
    panel, chunk = start.shape
    slopes = telemetry[...].astype(jnp.float32) * scales[...].astype(jnp.float32) / 128.0
    block[0:panel, :] = start[...]
    block[panel:, :] = slopes.astype(jnp.bfloat16)
    pieces = target.shape[1] // STEP
    for piece in range(pieces):
        part = slice(piece * STEP, (piece + 1) * STEP)
        side[piece * panel : (piece + 1) * panel, :] = target[:, part]
    rest = jnp.concatenate(
        [noise[:, piece * STEP : (piece + 1) * STEP] for piece in range(pieces)], axis=0
    )
    planes = []
    for _ in range(3):
        plane = rest.astype(jnp.bfloat16).astype(jnp.float32)
        rest = rest - plane
        planes.append(plane)
    planes.append(jnp.zeros_like(rest))
    side[pieces * panel :, :] = jnp.concatenate(planes, axis=0).astype(jnp.bfloat16)


def spot(row):
    return row + row // SUBAP * (2 * PAD) + PAD


def column(ref, begin, width, rows=slice(None)):
    return ref[rows, pl.ds(pl.multiple_of(begin, STEP), width)]


def moments(panel_ref, flat, sums):
    panel = 64
    local = (lax.broadcasted_iota(jnp.int32, (panel, STEP), 1) - STEP // 2).astype(jnp.float32)
    for sensor in range(sums.shape[0]):
        begins = [padded_start(sensor) + t * STEP for t in range(SUBAP // STEP)]
        dots = []
        for begin in begins:
            x = panel_ref[0:panel, begin : begin + STEP]
            xq = (x.astype(jnp.float32) * local).astype(jnp.bfloat16)
            dots.append(
                jnp.dot(
                    jnp.concatenate([x, xq], axis=0),
                    flat[begin : begin + STEP, :],
                    preferred_element_type=jnp.float32,
                )
            )
        plain = jnp.zeros((panel, 128), jnp.float32)
        moved = jnp.zeros((panel, 128), jnp.float32)
        for t, both in enumerate(dots):
            sums[sensor, t, 0:panel, :] = plain
            sums[sensor, t, panel:, :] = moved
            plain = plain + both[0:panel]
            moved = moved + (both[panel:] + both[0:panel] * float(t * STEP + STEP // 2))
        sums[sensor, SUBAP // STEP, 0:panel, :] = plain
        sums[sensor, SUBAP // STEP, panel:, :] = moved


def fill_ramp(ramp):
    rows = lax.broadcasted_iota(jnp.int32, ramp.shape, 0)
    cols = lax.broadcasted_iota(jnp.int32, ramp.shape, 1)
    ramp[...] = (rows - cols).astype(jnp.float32)


def padded_start(sensor):
    return sensor * (SUBAP + 2 * PAD) + PAD


def clear_pads(ref, axis, sensors):
    for sensor in range(sensors):
        for begin in (padded_start(sensor) - PAD, padded_start(sensor) + SUBAP):
            if axis:
                ref[:, begin : begin + PAD] = jnp.zeros((ref.shape[0], PAD), ref.dtype)
            else:
                ref[begin : begin + PAD, :] = jnp.zeros((PAD, ref.shape[1]), ref.dtype)


def keep_slopes(wide, base, height, own_slopes, at):
    panel = wide.shape[0] // 2
    own_slopes[0:panel, at : at + height] = jnp.zeros((panel, height), own_slopes.dtype)
    own_slopes[panel:, at : at + height] = column(wide, spot(base), height, slice(panel, None))


def edges(place, width):
    low = jnp.minimum((place - width) & -STEP, place - PAD)
    high = jnp.maximum((place + width) & -STEP, place + EDGE)
    return low, high


def widths(bands, sensor, sensors):
    return [bands[jnp.minimum(sensor, b), jnp.maximum(sensor, b)] for b in range(sensors)]


def list_jobs(bands, bases, height, sensors, jobs):
    number = jnp.int32(0)
    for group, base in enumerate(bases):
        sensor = base // SUBAP
        for b, width in enumerate(widths(bands, sensor, sensors)):
            for k in range(height // EDGE):
                place = base - sensor * SUBAP + k * EDGE
                low, high = edges(place, width)
                for begin, wanted in ((low, low + PAD > 0), (high, high < SUBAP)):
                    jobs[0, number] = group * (height // EDGE) + k
                    jobs[1, number] = begin + padded_start(b)
                    jobs[2, number] = begin - place
                    jobs[3, number] = width
                    number = number + wanted.astype(jnp.int32)
    for fill in range(ROUND - 1):
        for field, value in enumerate((0, 0, 0, 1)):
            jobs[field, number + fill] = value
    return (number + (ROUND - 1)) // ROUND


def near_and_far(
    base, group, norm_count, bands, panel_ref, flat, own_slopes, sums, ramp, noise, acc, saved, fresh
):
    panel = acc.shape[1]
    scale = 1.0 / norm_count
    sensors = sums.shape[0]
    sensor = base // SUBAP
    count = noise.shape[1] // EDGE
    local = (lax.broadcasted_iota(jnp.int32, (1, EDGE), 1) - EDGE // 2).astype(jnp.float32)
    width = widths(bands, sensor, sensors)
    rates = [1.0 / jnp.full((1, EDGE), w.astype(jnp.float32)) for w in width]
    places = [base - sensor * SUBAP + k * EDGE for k in range(count)]
    slopes = [column(own_slopes, (group * count + k) * EDGE, EDGE) for k in range(count)]
    begins = [[pl.multiple_of(padded_start(b) + p, STEP) for b in range(sensors)] for p in places]
    if fresh:
        raws = [
            jnp.dot(
                jnp.concatenate([flat[pl.ds(begin, EDGE), :] for begin in begins[k]], axis=0),
                slopes[k],
                preferred_element_type=jnp.float32,
            )
            for k in range(count)
        ]
    fars = []
    for k in range(count):
        near = jnp.zeros((panel, 128), jnp.float32)
        tilt = jnp.zeros((panel, 128), jnp.float32)
        middle = (places[k] + EDGE // 2).astype(jnp.float32)
        for b in range(sensors):
            low, high = edges(places[k], width[b])
            rate = rates[b][:, 0:128]
            at = [
                jnp.maximum(low + PAD, 0) // STEP,
                places[k] // STEP,
                (places[k] + EDGE) // STEP,
                jnp.minimum(high, SUBAP) // STEP,
            ]
            zero = [sums[b, t, 0:panel, :] for t in at]
            one = [sums[b, t, panel:, :] for t in at]
            left, right = zero[1] - zero[0], zero[3] - zero[2]
            left_q, right_q = one[1] - one[0], one[3] - one[2]
            near += left + right + rate * ((left_q - middle * left) - (right_q - middle * right))
            tilt += rate * (right - left)
        mix = jnp.concatenate([near, tilt], axis=0) * scale
        mix_high = mix.astype(jnp.bfloat16)
        mix_low = (mix - mix_high.astype(jnp.float32)).astype(jnp.bfloat16)
        far = jnp.dot(
            jnp.concatenate([mix_high, mix_low], axis=0), slopes[k], preferred_element_type=jnp.float32
        )
        fars.append(far[0 : 2 * panel] + far[2 * panel :])
    entries = []
    if fresh:
        square = ramp[0:EDGE, :]
        for k in range(count):
            line = noise[:, k * EDGE : (k + 1) * EDGE]
            for b in range(sensors):
                taper = jnp.maximum(0.0, scale - jnp.abs(square) * (rates[b] * scale))
                same = (sensor == b).astype(jnp.float32)
                entry = taper * raws[k][b * EDGE : (b + 1) * EDGE]
                entry = entry + jnp.where(square == 0.0, line * same, 0.0)
                entries.append(entry.astype(jnp.bfloat16))
                if saved is not None:
                    saved[k * sensors + b] = entries[-1]
    else:
        entries = [saved[n] for n in range(count * sensors)]
    for k in range(count):
        total = fars[k][0:panel] + local * fars[k][panel:]
        for b in range(sensors):
            total += jnp.dot(
                column(panel_ref, begins[k][b], EDGE, slice(0, panel)),
                entries[k * sensors + b],
                preferred_element_type=jnp.float32,
            )
        acc[group * count + k] = total


def run_jobs(rounds, norm_count, panel_ref, flat, own_slopes, ramp, jobs, acc, saved, fresh):
    panel = acc.shape[1]
    scale = 1.0 / norm_count
    kept = saved.shape[0] - ROUND

    def body(step, _):
        picked = [[jobs[field, step * ROUND + u] for field in range(4)] for u in range(ROUND)]
        begins = [pl.multiple_of(job[1], STEP) for job in picked]
        if fresh:
            raws = [
                jnp.dot(
                    flat[pl.ds(begin, PAD), :],
                    column(own_slopes, job[0] * EDGE, EDGE),
                    preferred_element_type=jnp.float32,
                )
                for job, begin in zip(picked, begins)
            ]
            entries = []
            for u, ((tile, begin, gap, width), raw) in enumerate(zip(picked, raws)):
                fall = scale / jnp.full((1, EDGE), width.astype(jnp.float32))
                taper = jnp.maximum(0.0, scale - jnp.abs(ramp[...] + gap.astype(jnp.float32)) * fall)
                entries.append((taper * raw).astype(jnp.bfloat16))
                saved[jnp.minimum(step * ROUND, kept) + u] = entries[-1]
        else:
            entries = [saved[step * ROUND + u] for u in range(ROUND)]
        parts = [
            jnp.dot(
                column(panel_ref, begin, PAD, slice(0, panel)), entry, preferred_element_type=jnp.float32
            )
            for begin, entry in zip(begins, entries)
        ]
        for job, part in zip(picked, parts):
            acc[job[0]] += part
        return 0

    lax.fori_loop(0, rounds, body, 0)


def first_kernel(sizes, bands_in, *refs):
    rows_n, cols_n, chunk, height, panel, norm_count, hops = sizes
    half = rows_n // 2
    mine, other = refs[:half], refs[half : 2 * half]
    sides = refs[2 * half]
    wide, flat, low, first, weight, saved_near, saved_jobs = refs[2 * half + 1 : 2 * half + 8]
    sums, noises, acc, ramp, own_slopes, bands, jobs, done = refs[2 * half + 8 :]
    lend = pltpu.make_async_copy(bands_in, bands, done)
    lend.start()
    sensors = sums.shape[0]
    col_id, row_id = lax.axis_index("col"), lax.axis_index("row")
    core = row_id % 2
    own = row_id // 2
    clear_pads(wide, 1, sensors)
    clear_pads(flat, 0, sensors)
    starts = [spot((hop ^ col_id) * (rows_n * chunk)) for hop in hops]
    pieces = height // STEP
    per_side = pieces * panel + 16
    for j in range(half):
        pos = own ^ j
        for source, parity in ((mine[j], core), (other[j], 1 - core)):
            shift = (2 * pos + parity) * chunk
            for slot in range(cols_n):
                place = pl.multiple_of(starts[slot] + shift, STEP)
                part = source[slot * chunk : (slot + 1) * chunk, :]
                wide[:, pl.ds(place, chunk)] = part
                flat[pl.ds(place, chunk), :] = part.T
        planes = sides[(j + 1) * per_side - 16 : (j + 1) * per_side, :].astype(jnp.float32)
        lines = planes[0:pieces] + planes[pieces : 2 * pieces] + planes[2 * pieces : 3 * pieces]
        noises[j, 0:1, :] = jnp.concatenate([lines[t : t + 1] for t in range(pieces)], axis=1)
    moments(wide, flat, sums)
    fill_ramp(ramp)
    bases = [(2 * (own ^ j) + core) * height for j in range(half)]
    for j in range(half):
        keep_slopes(wide, bases[j], height, own_slopes, j * height)
    lend.wait()
    rounds = list_jobs(bands, bases, height, sensors, jobs)

    for j in range(half):
        near_and_far(
            bases[j],
            j,
            norm_count,
            bands,
            wide,
            flat,
            own_slopes,
            sums,
            ramp,
            noises[j, 0:1, :],
            acc,
            saved_near if j == 0 else None,
            True,
        )
    run_jobs(rounds, norm_count, wide, flat, own_slopes, ramp, jobs, acc, saved_jobs, True)
    for j in range(half):
        for k in range(height // EDGE):
            part = slice(k * EDGE, (k + 1) * EDGE)
            both = column(wide, spot(bases[j]) + k * EDGE, EDGE).astype(jnp.float32)
            power = jnp.sum(both[panel:] * both[panel:], axis=0, keepdims=True)
            wgt = damping / (power / norm_count + noises[j, 0:1, part])
            goal = jnp.concatenate(
                [
                    sides[j * per_side + t * panel : j * per_side + (t + 1) * panel, :]
                    for t in range(k * EDGE // STEP, (k + 1) * EDGE // STEP)
                ],
                axis=1,
            ).astype(jnp.float32)
            new = both[0:panel] + wgt * (goal - acc[j * (height // EDGE) + k])
            if j == 0:
                first[:, part] = new
                weight[:, part] = jnp.broadcast_to(wgt, (8, EDGE))
            into = pl.multiple_of((own ^ j) * height + k * EDGE, EDGE)
            low[:, pl.ds(into, EDGE)] = new.astype(jnp.bfloat16)


def second_kernel(sizes, bands_in, wide, flat, home, away, first, weight, target, *refs):
    saved_near, saved_jobs, second, first_out, new, sums, acc, own_slopes, bands, jobs, done = refs
    rows_n, cols_n, chunk, height, panel, norm_count, hops = sizes
    lend = pltpu.make_async_copy(bands_in, bands, done.at[0])
    lend.start()
    give = pltpu.make_async_copy(first, first_out, done.at[1])
    give.start()
    sensors = sums.shape[0]
    row_id = lax.axis_index("row")
    core = row_id % 2
    clear_pads(new, 1, sensors)
    for pos in range(rows_n // 2):
        for source, parity in ((home, core), (away, 1 - core)):
            place = pl.multiple_of(spot((2 * pos + parity) * height), STEP)
            new[:, pl.ds(place, height)] = source[:, pos * height : (pos + 1) * height]
    moments(new, flat, sums)
    base = row_id * height
    keep_slopes(wide, base, height, own_slopes, 0)
    lend.wait()
    rounds = list_jobs(bands, [base], height, sensors, jobs)
    near_and_far(
        base, 0, norm_count, bands, new, flat, own_slopes, sums, None, weight, acc, saved_near, False
    )
    run_jobs(rounds, norm_count, new, flat, own_slopes, None, jobs, acc, saved_jobs, False)
    for k in range(height // EDGE):
        part = slice(k * EDGE, (k + 1) * EDGE)
        goal = target[:, part].astype(jnp.float32)
        second[:, part] = first[:, part] + weight[0:1, part] * (goal - acc[k])
    give.wait()


def flip(block, axis, bit):
    size = lax.axis_size(axis)
    return lax.ppermute(block, axis, [(i, i ^ bit) for i in range(size)])


def gathered_plan(telemetry, scales, bands, noise, start, target):
    rows_n = lax.axis_size("row")
    cols_n = lax.axis_size("col")
    chunk, frames = telemetry.shape
    height, panel = target.shape
    order = chunk * rows_n * cols_n
    sensors = order // SUBAP
    padded = order + 2 * PAD * sensors
    half = rows_n // 2
    vmem = pl.BlockSpec(memory_space=pltpu.VMEM)
    params = pltpu.CompilerParams(vmem_limit_bytes=24 * 1024 * 1024)
    noise = noise.reshape(1, height)
    target = target.T
    own = (telemetry.T, scales.reshape(1, chunk), start.T, target, noise, bands)
    block, side, bands = pl.pallas_call(
        prepare_kernel,
        out_shape=(
            jax.ShapeDtypeStruct((2 * panel, chunk), jnp.bfloat16),
            jax.ShapeDtypeStruct((height // STEP * panel + 16, 128), jnp.bfloat16),
            jax.ShapeDtypeStruct(bands.shape, bands.dtype),
        ),
        in_specs=[pl.BlockSpec(memory_space=pltpu.HBM)] * len(own),
        out_specs=(vmem,) * 3,
        scratch_shapes=[pltpu.VMEM(x.shape, x.dtype) for x in own]
        + [pltpu.SemaphoreType.DMA((len(own),))],
        compiler_params=params,
        name="prepare",
    )(*[pltpu.with_memory_space_constraint(x, pltpu.HBM) for x in own])
    hops = (0,)
    bit = cols_n // 2
    while bit:
        block = jnp.concatenate([block, flip(block, "col", bit)], axis=0)
        hops = hops + tuple(hop ^ bit for hop in hops)
        bit //= 2
    bit = 2
    while bit < rows_n:
        side = jnp.concatenate([side, flip(side, "row", bit)], axis=0)
        bit *= 2
    sizes = (rows_n, cols_n, chunk, height, panel, float(order // 4), hops)
    mine = [block] + [flip(block, "row", 2 * j) for j in range(1, half)]
    other = [flip(part, "row", 1) for part in mine]
    tiles = height // EDGE
    sums = pltpu.VMEM((sensors, SUBAP // STEP + 1, 2 * panel, 128), jnp.float32)
    ramp = pltpu.VMEM((PAD, EDGE), jnp.float32)
    lent = pltpu.SMEM(bands.shape, bands.dtype)

    def scratch(groups):
        return [
            pltpu.VMEM((groups * tiles, panel, EDGE), jnp.float32),
            *([ramp] if groups > 1 else []),
            pltpu.VMEM((2 * panel, groups * height), jnp.bfloat16),
            lent,
            pltpu.SMEM((4, groups * tiles * sensors * 2 + ROUND), jnp.int32),
        ]

    wide, flat, low, first, weight, *saved = pl.pallas_call(
        functools.partial(first_kernel, sizes),
        out_shape=(
            jax.ShapeDtypeStruct((2 * panel, padded), jnp.bfloat16),
            jax.ShapeDtypeStruct((padded, 2 * panel), jnp.bfloat16),
            jax.ShapeDtypeStruct((panel, half * height), jnp.bfloat16),
            jax.ShapeDtypeStruct((panel, height), jnp.float32),
            jax.ShapeDtypeStruct((8, height), jnp.float32),
            jax.ShapeDtypeStruct((tiles * sensors, EDGE, EDGE), jnp.bfloat16),
            jax.ShapeDtypeStruct((tiles * sensors * 2 + ROUND, PAD, EDGE), jnp.bfloat16),
        ),
        in_specs=[vmem] * (2 + rows_n),
        out_specs=(vmem,) * 7,
        scratch_shapes=[sums, pltpu.VMEM((half, 8, height), jnp.float32)]
        + scratch(half)
        + [pltpu.SemaphoreType.DMA],
        compiler_params=params,
        name="first_pass",
    )(bands, *mine, *other, side)
    away = flip(low, "row", 1)
    second, first = pl.pallas_call(
        functools.partial(second_kernel, sizes),
        out_shape=(jax.ShapeDtypeStruct((panel, height), jnp.float32),) * 2,
        in_specs=[vmem] * 10,
        out_specs=(vmem, pl.BlockSpec(memory_space=pl.ANY)),
        scratch_shapes=[pltpu.VMEM((panel, padded), jnp.bfloat16), sums]
        + scratch(1)
        + [pltpu.SemaphoreType.DMA((2,))],
        compiler_params=params,
        name="second_pass",
    )(bands, wide, flat, low, away, first, weight, target, *saved)
    return (first.T, second.T)


def power_of_two(number):
    return number > 0 and number & (number - 1) == 0


def fits(mesh, telemetry, target):
    rows_n, cols_n = mesh.shape["row"], mesh.shape["col"]
    order, frames = telemetry.shape
    panel = target.shape[1]
    height = order // rows_n
    return (
        power_of_two(rows_n)
        and power_of_two(cols_n)
        and rows_n >= 2
        and frames == panel == 64
        and order % SUBAP == 0
        and SUBAP % height == 0
        and height == 2 * EDGE
        and order // (rows_n * cols_n) == STEP
        and order <= 2 * SUBAP
    )


def solution(mesh):
    def program(telemetry, scales, bands, noise, start, target):
        plan = gathered_plan if fits(mesh, telemetry, target) else tiled_plan
        return jax.shard_map(
            plan,
            mesh=mesh,
            in_specs=(
                P(("col", "row"), None),
                P(("col", "row")),
                P(),
                P("row"),
                P(("col", "row"), None),
                P("row", None),
            ),
            out_specs=(P("row", None), P("row", None)),
            check_vma=False,
        )(telemetry, scales, bands, noise, start, target)

    return program
```

```python
import functools
import math

import jax
import jax.numpy as jnp
from jax import lax
from jax.experimental import pallas as pl
from jax.experimental.pallas import tpu as pltpu
from jax.sharding import PartitionSpec as P

SUBAP = 2048


damping = 0.4


def from_root(block, axis, holder):
    block = jnp.where(lax.axis_index(axis) == holder, block, jnp.zeros_like(block))
    return lax.psum(block, axis)


def tiled_plan(telemetry, scales, bands, noise, start, target):
    frame_count = telemetry.shape[1]
    row_count = lax.axis_size("row")
    col_count = lax.axis_size("col")
    ratio = row_count // col_count
    row_id = lax.axis_index("row")
    col_id = lax.axis_index("col")
    order_total = telemetry.shape[0] * row_count * col_count
    norm_count = jnp.float32(order_total // 4)
    slopes = (telemetry.astype(jnp.float32) * scales.astype(jnp.float32)[:, None] / 128.0).astype(
        jnp.bfloat16
    )
    joined = jnp.concatenate([slopes, start], axis=1)
    col_joined = lax.all_gather(joined, "row", axis=0, tiled=True)
    col_width = col_joined.shape[0]
    row_height = col_width // ratio
    half = lax.dynamic_slice_in_dim(col_joined, row_id % ratio * row_height, row_height, 0)
    row_joined = from_root(half, "col", row_id // ratio)
    row_slopes = row_joined[:, :frame_count]
    row_start = row_joined[:, frame_count:]
    col_slopes = col_joined[:, :frame_count]
    col_start = col_joined[:, frame_count:]
    panel_width = col_start.shape[1]
    row_f = row_slopes.astype(jnp.float32)
    weight = damping / (jnp.sum(row_f * row_f, axis=1) / norm_count + noise)
    count = bands.shape[0]
    index = jnp.arange(count, dtype=jnp.int32)
    sym = jnp.where(index[:, None] <= index[None, :], bands, bands.T).astype(jnp.float32)
    row_ids = row_id * row_height + jnp.arange(row_height, dtype=jnp.int32)
    onehot = (row_ids[:, None] // SUBAP == index[None, :]).astype(jnp.float32)
    row_band = jnp.dot(onehot, sym, precision=lax.Precision.HIGHEST)
    row_pos = (row_ids % SUBAP).astype(jnp.float32)
    width = math.gcd(math.gcd(col_width, 512), SUBAP)
    nblocks = col_width // width

    def build(step, carry):
        tile, acc = carry
        offset = step * width
        cols = lax.dynamic_slice_in_dim(col_slopes, offset, width, 0)
        raw = (
            lax.dot_general(
                row_slopes, cols, (((1,), (1,)), ((), ())), preferred_element_type=jnp.float32
            )
            / norm_count
        )
        col_ids = col_id * col_width + offset + jnp.arange(width, dtype=jnp.int32)
        band = lax.dynamic_slice_in_dim(row_band, (col_id * col_width + offset) // SUBAP, 1, 1)
        dist = jnp.abs(row_pos[:, None] - (col_ids % SUBAP).astype(jnp.float32)[None, :])
        taper = jnp.maximum(0.0, 1.0 - dist / band)
        diag = jnp.where(row_ids[:, None] == col_ids[None, :], noise[:, None], jnp.float32(0.0))
        entry = (taper * raw + diag).astype(jnp.bfloat16)
        tile = lax.dynamic_update_slice_in_dim(tile, entry, offset, 1)
        return (tile, acc)

    tile_init = jnp.zeros((row_height, col_width), jnp.bfloat16)
    acc_init = jnp.zeros((row_height, panel_width), jnp.float32)
    tile, acc = lax.fori_loop(0, nblocks, build, (tile_init, acc_init))
    product0 = jnp.dot(tile, col_start, preferred_element_type=jnp.float32)
    target_f = target.astype(jnp.float32)

    def refine(current, product):
        share = lax.psum_scatter(product, "col", scatter_dimension=0, tiled=True)
        share_rows = row_height // col_count
        begin = col_id * share_rows
        cur_part = lax.dynamic_slice_in_dim(current, begin, share_rows, 0)
        tgt_part = lax.dynamic_slice_in_dim(target_f, begin, share_rows, 0)
        wgt_part = lax.dynamic_slice_in_dim(weight, begin, share_rows, 0)
        updated = cur_part + wgt_part[:, None] * (tgt_part - share)
        return lax.all_gather(updated, "col", axis=0, tiled=True)

    first = refine(row_start.astype(jnp.float32), product0)
    first_low = first.astype(jnp.bfloat16)
    pieces = [from_root(first_low, "row", col_id * ratio + offset_q) for offset_q in range(ratio)]
    col_first = jnp.concatenate(pieces, axis=0)
    product1 = jnp.dot(tile, col_first, preferred_element_type=jnp.float32)
    second = refine(first, product1)
    return (first, second)


EDGE = 256
STEP = 128
PAD = 384
ROUND = 4


def prepare_kernel(*refs):
    count = 6
    sources, (block, side, lent), copies = refs[:count], refs[count : count + 3], refs[count + 3 :]
    done = copies[count]
    moves = []
    for k in range(count):
        move = pltpu.make_async_copy(sources[k], copies[k], done.at[k])
        move.start()
        moves.append(move)
    for move in moves:
        move.wait()
    telemetry, scales, start, target, noise, bands = copies[:count]
    lent[...] = bands[...]
    panel, chunk = start.shape
    slopes = telemetry[...].astype(jnp.float32) * scales[...].astype(jnp.float32) / 128.0
    block[0:panel, :] = start[...]
    block[panel:, :] = slopes.astype(jnp.bfloat16)
    pieces = target.shape[1] // STEP
    for piece in range(pieces):
        part = slice(piece * STEP, (piece + 1) * STEP)
        side[piece * panel : (piece + 1) * panel, :] = target[:, part]
    rest = jnp.concatenate(
        [noise[:, piece * STEP : (piece + 1) * STEP] for piece in range(pieces)], axis=0
    )
    planes = []
    for _ in range(3):
        plane = rest.astype(jnp.bfloat16).astype(jnp.float32)
        rest = rest - plane
        planes.append(plane)
    planes.append(jnp.zeros_like(rest))
    side[pieces * panel :, :] = jnp.concatenate(planes, axis=0).astype(jnp.bfloat16)


def spot(row):
    return row + row // SUBAP * (2 * PAD) + PAD


def column(ref, begin, width, rows=slice(None)):
    return ref[rows, pl.ds(pl.multiple_of(begin, STEP), width)]


def moments(panel_ref, flat, sums):
    panel = 64
    local = (lax.broadcasted_iota(jnp.int32, (panel, STEP), 1) - STEP // 2).astype(jnp.float32)
    for sensor in range(sums.shape[0]):
        begins = [padded_start(sensor) + t * STEP for t in range(SUBAP // STEP)]
        dots = []
        for begin in begins:
            x = panel_ref[0:panel, begin : begin + STEP]
            xq = (x.astype(jnp.float32) * local).astype(jnp.bfloat16)
            dots.append(
                jnp.dot(
                    jnp.concatenate([x, xq], axis=0),
                    flat[begin : begin + STEP, :],
                    preferred_element_type=jnp.float32,
                )
            )
        plain = jnp.zeros((panel, 128), jnp.float32)
        moved = jnp.zeros((panel, 128), jnp.float32)
        for t, both in enumerate(dots):
            sums[sensor, t, 0:panel, :] = plain
            sums[sensor, t, panel:, :] = moved
            plain = plain + both[0:panel]
            moved = moved + (both[panel:] + both[0:panel] * float(t * STEP + STEP // 2))
        sums[sensor, SUBAP // STEP, 0:panel, :] = plain
        sums[sensor, SUBAP // STEP, panel:, :] = moved


def fill_ramp(ramp):
    rows = lax.broadcasted_iota(jnp.int32, ramp.shape, 0)
    cols = lax.broadcasted_iota(jnp.int32, ramp.shape, 1)
    ramp[...] = (rows - cols).astype(jnp.float32)


def padded_start(sensor):
    return sensor * (SUBAP + 2 * PAD) + PAD


def clear_pads(ref, axis, sensors):
    for sensor in range(sensors):
        for begin in (padded_start(sensor) - PAD, padded_start(sensor) + SUBAP):
            if axis:
                ref[:, begin : begin + PAD] = jnp.zeros((ref.shape[0], PAD), ref.dtype)
            else:
                ref[begin : begin + PAD, :] = jnp.zeros((PAD, ref.shape[1]), ref.dtype)


def keep_slopes(wide, base, height, own_slopes, at):
    panel = wide.shape[0] // 2
    own_slopes[0:panel, at : at + height] = jnp.zeros((panel, height), own_slopes.dtype)
    own_slopes[panel:, at : at + height] = column(wide, spot(base), height, slice(panel, None))


def edges(place, width):
    slim = (width & (STEP - 1)) == 0
    span = jnp.where(slim, EDGE, PAD)
    low = jnp.minimum((place - width) & -STEP, place - span)
    high = jnp.maximum((place + width) & -STEP, place + EDGE)
    return low, high, span, slim.astype(jnp.int32)


def widths(bands, sensor, sensors):
    return [bands[jnp.minimum(sensor, b), jnp.maximum(sensor, b)] for b in range(sensors)]


def list_jobs(bands, bases, height, sensors, jobs):
    number = [jnp.int32(0), jnp.int32(0)]
    for group, base in enumerate(bases):
        sensor = base // SUBAP
        for b, width in enumerate(widths(bands, sensor, sensors)):
            for k in range(height // EDGE):
                place = base - sensor * SUBAP + k * EDGE
                low, high, span, slim = edges(place, width)
                for begin, wanted in ((low, low + span > 0), (high, high < SUBAP)):
                    at = jnp.where(slim == 1, number[1], number[0])
                    jobs[slim, 0, at] = group * (height // EDGE) + k
                    jobs[slim, 1, at] = begin + padded_start(b)
                    jobs[slim, 2, at] = begin - place
                    jobs[slim, 3, at] = width
                    one = wanted.astype(jnp.int32)
                    number = [number[0] + one * (1 - slim), number[1] + one * slim]
    for kind in range(2):
        for fill in range(ROUND - 1):
            for field, value in enumerate((0, 0, 0, 1)):
                jobs[kind, field, number[kind] + fill] = value
    return [(count + (ROUND - 1)) // ROUND for count in number]


def near_and_far(
    base, group, norm_count, bands, panel_ref, flat, own_slopes, sums, ramp, noise, acc, saved, fresh
):
    panel = acc.shape[1]
    scale = 1.0 / norm_count
    sensors = sums.shape[0]
    sensor = base // SUBAP
    count = noise.shape[1] // EDGE
    local = (lax.broadcasted_iota(jnp.int32, (1, EDGE), 1) - EDGE // 2).astype(jnp.float32)
    width = widths(bands, sensor, sensors)
    rates = [1.0 / jnp.full((1, EDGE), w.astype(jnp.float32)) for w in width]
    places = [base - sensor * SUBAP + k * EDGE for k in range(count)]
    slopes = [column(own_slopes, (group * count + k) * EDGE, EDGE) for k in range(count)]
    begins = [[pl.multiple_of(padded_start(b) + p, STEP) for b in range(sensors)] for p in places]
    if fresh:
        raws = [
            jnp.dot(
                jnp.concatenate([flat[pl.ds(begin, EDGE), :] for begin in begins[k]], axis=0),
                slopes[k],
                preferred_element_type=jnp.float32,
            )
            for k in range(count)
        ]
    fars = []
    for k in range(count):
        near = jnp.zeros((panel, 128), jnp.float32)
        tilt = jnp.zeros((panel, 128), jnp.float32)
        middle = (places[k] + EDGE // 2).astype(jnp.float32)
        for b in range(sensors):
            low, high, span, _ = edges(places[k], width[b])
            rate = rates[b][:, 0:128]
            at = [
                jnp.maximum(low + span, 0) // STEP,
                places[k] // STEP,
                (places[k] + EDGE) // STEP,
                jnp.minimum(high, SUBAP) // STEP,
            ]
            zero = [sums[b, t, 0:panel, :] for t in at]
            one = [sums[b, t, panel:, :] for t in at]
            left, right = zero[1] - zero[0], zero[3] - zero[2]
            left_q, right_q = one[1] - one[0], one[3] - one[2]
            near += left + right + rate * ((left_q - middle * left) - (right_q - middle * right))
            tilt += rate * (right - left)
        mix = jnp.concatenate([near, tilt], axis=0) * scale
        mix_high = mix.astype(jnp.bfloat16)
        mix_low = (mix - mix_high.astype(jnp.float32)).astype(jnp.bfloat16)
        far = jnp.dot(
            jnp.concatenate([mix_high, mix_low], axis=0), slopes[k], preferred_element_type=jnp.float32
        )
        fars.append(far[0 : 2 * panel] + far[2 * panel :])
    entries = []
    if fresh:
        square = ramp[0:EDGE, :]
        for k in range(count):
            line = noise[:, k * EDGE : (k + 1) * EDGE]
            for b in range(sensors):
                taper = jnp.maximum(0.0, scale - jnp.abs(square) * (rates[b] * scale))
                same = (sensor == b).astype(jnp.float32)
                entry = taper * raws[k][b * EDGE : (b + 1) * EDGE]
                entry = entry + jnp.where(square == 0.0, line * same, 0.0)
                entries.append(entry.astype(jnp.bfloat16))
                if saved is not None:
                    saved[k * sensors + b] = entries[-1]
    else:
        entries = [saved[n] for n in range(count * sensors)]
    for k in range(count):
        total = fars[k][0:panel] + local * fars[k][panel:]
        for b in range(sensors):
            total += jnp.dot(
                column(panel_ref, begins[k][b], EDGE, slice(0, panel)),
                entries[k * sensors + b],
                preferred_element_type=jnp.float32,
            )
        acc[group * count + k] = total


def run_jobs(rounds, norm_count, panel_ref, flat, own_slopes, ramp, jobs, acc, saved, fresh):
    panel = acc.shape[1]
    scale = 1.0 / norm_count

    def body(kind, step):
        span = saved[kind].shape[1]
        kept = saved[kind].shape[0] - ROUND
        picked = [[jobs[kind, field, step * ROUND + u] for field in range(4)] for u in range(ROUND)]
        begins = [pl.multiple_of(job[1], STEP) for job in picked]
        if fresh:
            raws = [
                jnp.dot(
                    flat[pl.ds(begin, span), :],
                    column(own_slopes, job[0] * EDGE, EDGE),
                    preferred_element_type=jnp.float32,
                )
                for job, begin in zip(picked, begins)
            ]
            entries = []
            for u, ((tile, begin, gap, width), raw) in enumerate(zip(picked, raws)):
                fall = scale / jnp.full((1, EDGE), width.astype(jnp.float32))
                away = jnp.abs(ramp[0:span, :] + gap.astype(jnp.float32))
                taper = jnp.maximum(0.0, scale - away * fall)
                entries.append((taper * raw).astype(jnp.bfloat16))
                saved[kind][jnp.minimum(step * ROUND, kept) + u] = entries[-1]
        else:
            entries = [saved[kind][step * ROUND + u] for u in range(ROUND)]
        parts = [
            jnp.dot(
                column(panel_ref, begin, span, slice(0, panel)), entry, preferred_element_type=jnp.float32
            )
            for begin, entry in zip(begins, entries)
        ]
        for job, part in zip(picked, parts):
            acc[job[0]] += part

    for kind in range(2):

        def step(count, _, kind=kind):
            body(kind, count)
            return 0

        lax.fori_loop(0, rounds[kind], step, 0)


def place_parts(sizes, parts, wide, flat):
    rows_n, cols_n, chunk, height, panel, norm_count, hops = sizes
    col_id, row_id = lax.axis_index("col"), lax.axis_index("row")
    core = row_id % 2
    own = row_id // 2
    starts = [spot((hop ^ col_id) * (rows_n * chunk)) for hop in hops]
    for j, near, source in parts:
        shift = (2 * (own ^ j) + (core if near else 1 - core)) * chunk
        for slot in range(cols_n):
            place = pl.multiple_of(starts[slot] + shift, STEP)
            part = source[slot * chunk : (slot + 1) * chunk, :]
            wide[:, pl.ds(place, chunk)] = part
            flat[pl.ds(place, chunk), :] = part.T


def place_kernel(sizes, which, fresh, *refs):
    count = len(which)
    wide, flat = refs[-2:]
    if fresh:
        sensors = wide.shape[1] // (SUBAP + 2 * PAD)
        clear_pads(wide, 1, sensors)
        clear_pads(flat, 0, sensors)
    sources = refs[len(refs) - 2 - count : len(refs) - 2]
    place_parts(sizes, [(j, near, source) for (j, near), source in zip(which, sources)], wide, flat)


def first_kernel(sizes, which, bands_in, *refs):
    rows_n, cols_n, chunk, height, panel, norm_count, hops = sizes
    half = rows_n // 2
    sources, sides = refs[2 : 2 + len(which)], refs[2 + len(which)]
    refs = refs[3 + len(which) :]
    wide, flat, low, first, weight, saved_near, *saved_jobs = refs[:8]
    sums, noises, acc, ramp, own_slopes, bands, jobs, done = refs[8:]
    lend = pltpu.make_async_copy(bands_in, bands, done)
    lend.start()
    sensors = sums.shape[0]
    row_id = lax.axis_index("row")
    core = row_id % 2
    own = row_id // 2
    pieces = height // STEP
    per_side = pieces * panel + 16
    place_parts(sizes, [(j, near, source) for (j, near), source in zip(which, sources)], wide, flat)
    for j in range(half):
        planes = sides[(j + 1) * per_side - 16 : (j + 1) * per_side, :].astype(jnp.float32)
        lines = planes[0:pieces] + planes[pieces : 2 * pieces] + planes[2 * pieces : 3 * pieces]
        noises[j, 0:1, :] = jnp.concatenate([lines[t : t + 1] for t in range(pieces)], axis=1)
    moments(wide, flat, sums)
    fill_ramp(ramp)
    bases = [(2 * (own ^ j) + core) * height for j in range(half)]
    for j in range(half):
        keep_slopes(wide, bases[j], height, own_slopes, j * height)
    lend.wait()

    for j in range(half):
        near_and_far(
            bases[j],
            j,
            norm_count,
            bands,
            wide,
            flat,
            own_slopes,
            sums,
            ramp,
            noises[j, 0:1, :],
            acc,
            saved_near if j == 0 else None,
            True,
        )
    rounds = list_jobs(bands, bases, height, sensors, jobs)
    run_jobs(rounds, norm_count, wide, flat, own_slopes, ramp, jobs, acc, saved_jobs, True)
    for j in range(half):
        for k in range(height // EDGE):
            part = slice(k * EDGE, (k + 1) * EDGE)
            both = column(wide, spot(bases[j]) + k * EDGE, EDGE).astype(jnp.float32)
            power = jnp.sum(both[panel:] * both[panel:], axis=0, keepdims=True)
            wgt = damping / (power / norm_count + noises[j, 0:1, part])
            goal = jnp.concatenate(
                [
                    sides[j * per_side + t * panel : j * per_side + (t + 1) * panel, :]
                    for t in range(k * EDGE // STEP, (k + 1) * EDGE // STEP)
                ],
                axis=1,
            ).astype(jnp.float32)
            new = both[0:panel] + wgt * (goal - acc[j * (height // EDGE) + k])
            if j == 0:
                first[:, part] = new
                weight[:, part] = jnp.broadcast_to(wgt, (8, EDGE))
            into = pl.multiple_of((own ^ j) * height + k * EDGE, EDGE)
            low[:, pl.ds(into, EDGE)] = new.astype(jnp.bfloat16)


def second_kernel(sizes, bands_in, wide, flat, home, away, first, weight, target, *refs):
    saved_near, *saved_jobs = refs[:3]
    second, first_out, new, sums, acc, own_slopes, bands, jobs, done = refs[3:]
    rows_n, cols_n, chunk, height, panel, norm_count, hops = sizes
    lend = pltpu.make_async_copy(bands_in, bands, done.at[0])
    lend.start()
    give = pltpu.make_async_copy(first, first_out, done.at[1])
    give.start()
    sensors = sums.shape[0]
    row_id = lax.axis_index("row")
    core = row_id % 2
    clear_pads(new, 1, sensors)
    for pos in range(rows_n // 2):
        for source, parity in ((home, core), (away, 1 - core)):
            place = pl.multiple_of(spot((2 * pos + parity) * height), STEP)
            new[:, pl.ds(place, height)] = source[:, pos * height : (pos + 1) * height]
    moments(new, flat, sums)
    base = row_id * height
    keep_slopes(wide, base, height, own_slopes, 0)
    lend.wait()
    rounds = list_jobs(bands, [base], height, sensors, jobs)
    near_and_far(
        base, 0, norm_count, bands, new, flat, own_slopes, sums, None, weight, acc, saved_near, False
    )
    run_jobs(rounds, norm_count, new, flat, own_slopes, None, jobs, acc, saved_jobs, False)
    for k in range(height // EDGE):
        part = slice(k * EDGE, (k + 1) * EDGE)
        goal = target[:, part].astype(jnp.float32)
        second[:, part] = first[:, part] + weight[0:1, part] * (goal - acc[k])
    give.wait()


def flip(block, axis, bit):
    size = lax.axis_size(axis)
    return lax.ppermute(block, axis, [(i, i ^ bit) for i in range(size)])


def gathered_plan(telemetry, scales, bands, noise, start, target):
    rows_n = lax.axis_size("row")
    cols_n = lax.axis_size("col")
    chunk, frames = telemetry.shape
    height, panel = target.shape
    order = chunk * rows_n * cols_n
    sensors = order // SUBAP
    padded = order + 2 * PAD * sensors
    half = rows_n // 2
    vmem = pl.BlockSpec(memory_space=pltpu.VMEM)
    params = pltpu.CompilerParams(vmem_limit_bytes=24 * 1024 * 1024)
    noise = noise.reshape(1, height)
    target = target.T
    own = (telemetry.T, scales.reshape(1, chunk), start.T, target, noise, bands)
    block, side, bands = pl.pallas_call(
        prepare_kernel,
        out_shape=(
            jax.ShapeDtypeStruct((2 * panel, chunk), jnp.bfloat16),
            jax.ShapeDtypeStruct((height // STEP * panel + 16, 128), jnp.bfloat16),
            jax.ShapeDtypeStruct(bands.shape, bands.dtype),
        ),
        in_specs=[pl.BlockSpec(memory_space=pltpu.HBM)] * len(own),
        out_specs=(vmem,) * 3,
        scratch_shapes=[pltpu.VMEM(x.shape, x.dtype) for x in own]
        + [pltpu.SemaphoreType.DMA((len(own),))],
        compiler_params=params,
        name="prepare",
    )(*[pltpu.with_memory_space_constraint(x, pltpu.HBM) for x in own])
    hops = (0,)
    bit = cols_n // 2
    while bit:
        block = jnp.concatenate([block, flip(block, "col", bit)], axis=0)
        hops = hops + tuple(hop ^ bit for hop in hops)
        bit //= 2
    bit = 2
    while bit < rows_n:
        side = jnp.concatenate([side, flip(side, "row", bit)], axis=0)
        bit *= 2
    sizes = (rows_n, cols_n, chunk, height, panel, float(order // 4), hops)
    mine = [block] + [flip(block, "row", 2 * j) for j in range(1, half)]
    other = [flip(part, "row", 1) for part in mine]
    tiles = height // EDGE
    sums = pltpu.VMEM((sensors, SUBAP // STEP + 1, 2 * panel, 128), jnp.float32)
    ramp = pltpu.VMEM((PAD, EDGE), jnp.float32)
    lent = pltpu.SMEM(bands.shape, bands.dtype)

    def scratch(groups):
        return [
            pltpu.VMEM((groups * tiles, panel, EDGE), jnp.float32),
            *([ramp] if groups > 1 else []),
            pltpu.VMEM((2 * panel, groups * height), jnp.bfloat16),
            lent,
            pltpu.SMEM((2, 4, groups * tiles * sensors * 2 + ROUND), jnp.int32),
        ]

    placed = (
        jax.ShapeDtypeStruct((2 * panel, padded), jnp.bfloat16),
        jax.ShapeDtypeStruct((padded, 2 * panel), jnp.bfloat16),
    )

    def place(which, before):
        parts = [mine[j] if near else other[j] for j, near in which]
        return pl.pallas_call(
            functools.partial(place_kernel, sizes, which, not before),
            out_shape=placed,
            in_specs=[vmem] * (len(before) + len(parts)),
            out_specs=(vmem,) * 2,
            input_output_aliases={k: k for k in range(len(before))},
            compiler_params=params,
            name="place",
        )(*before, *parts)

    everything = [(j, near) for j in range(half) for near in (True, False)]
    early = [[(0, True), (0, False)], [(1, True), (2, True), (3, True)]]
    arrays = ()
    for which in early:
        arrays = place(which, arrays)
    late = [pair for pair in everything if pair not in sum(early, [])]
    wide, flat, low, first, weight, *saved = pl.pallas_call(
        functools.partial(first_kernel, sizes, late),
        out_shape=placed
        + (
            jax.ShapeDtypeStruct((panel, half * height), jnp.bfloat16),
            jax.ShapeDtypeStruct((panel, height), jnp.float32),
            jax.ShapeDtypeStruct((8, height), jnp.float32),
            jax.ShapeDtypeStruct((tiles * sensors, EDGE, EDGE), jnp.bfloat16),
            jax.ShapeDtypeStruct((tiles * sensors * 2 + ROUND, PAD, EDGE), jnp.bfloat16),
            jax.ShapeDtypeStruct((tiles * sensors * 2 + ROUND, EDGE, EDGE), jnp.bfloat16),
        ),
        in_specs=[vmem] * (4 + len(late)),
        out_specs=(vmem,) * 8,
        input_output_aliases={1: 0, 2: 1},
        scratch_shapes=[sums, pltpu.VMEM((half, 8, height), jnp.float32)]
        + scratch(half)
        + [pltpu.SemaphoreType.DMA],
        compiler_params=params,
        name="first_pass",
    )(bands, *arrays, *[mine[j] if near else other[j] for j, near in late], side)
    away = flip(low, "row", 1)
    second, first = pl.pallas_call(
        functools.partial(second_kernel, sizes),
        out_shape=(jax.ShapeDtypeStruct((panel, height), jnp.float32),) * 2,
        in_specs=[vmem] * 11,
        out_specs=(vmem, pl.BlockSpec(memory_space=pl.ANY)),
        scratch_shapes=[pltpu.VMEM((panel, padded), jnp.bfloat16), sums]
        + scratch(1)
        + [pltpu.SemaphoreType.DMA((2,))],
        compiler_params=params,
        name="second_pass",
    )(bands, wide, flat, low, away, first, weight, target, *saved)
    return (first.T, second.T)


def power_of_two(number):
    return number > 0 and number & (number - 1) == 0


def fits(mesh, telemetry, target):
    rows_n, cols_n = mesh.shape["row"], mesh.shape["col"]
    order, frames = telemetry.shape
    panel = target.shape[1]
    height = order // rows_n
    return (
        power_of_two(rows_n)
        and power_of_two(cols_n)
        and rows_n >= 2
        and frames == panel == 64
        and order % SUBAP == 0
        and SUBAP % height == 0
        and height == 2 * EDGE
        and order // (rows_n * cols_n) == STEP
        and order <= 2 * SUBAP
    )


def solution(mesh):
    def program(telemetry, scales, bands, noise, start, target):
        plan = gathered_plan if fits(mesh, telemetry, target) else tiled_plan
        return jax.shard_map(
            plan,
            mesh=mesh,
            in_specs=(
                P(("col", "row"), None),
                P(("col", "row")),
                P(),
                P("row"),
                P(("col", "row"), None),
                P("row", None),
            ),
            out_specs=(P("row", None), P("row", None)),
            check_vma=False,
        )(telemetry, scales, bands, noise, start, target)

    return program
```

```python
import functools
import math

import jax
import jax.numpy as jnp
from jax import lax
from jax.experimental import pallas as pl
from jax.experimental.pallas import tpu as pltpu
from jax.sharding import PartitionSpec as P

SUBAP = 2048


damping = 0.4


def from_root(block, axis, holder):
    block = jnp.where(lax.axis_index(axis) == holder, block, jnp.zeros_like(block))
    return lax.psum(block, axis)


def tiled_plan(telemetry, scales, bands, noise, start, target):
    frame_count = telemetry.shape[1]
    row_count = lax.axis_size("row")
    col_count = lax.axis_size("col")
    ratio = row_count // col_count
    row_id = lax.axis_index("row")
    col_id = lax.axis_index("col")
    order_total = telemetry.shape[0] * row_count * col_count
    norm_count = jnp.float32(order_total // 4)
    slopes = (telemetry.astype(jnp.float32) * scales.astype(jnp.float32)[:, None] / 128.0).astype(
        jnp.bfloat16
    )
    joined = jnp.concatenate([slopes, start], axis=1)
    col_joined = lax.all_gather(joined, "row", axis=0, tiled=True)
    col_width = col_joined.shape[0]
    row_height = col_width // ratio
    half = lax.dynamic_slice_in_dim(col_joined, row_id % ratio * row_height, row_height, 0)
    row_joined = from_root(half, "col", row_id // ratio)
    row_slopes = row_joined[:, :frame_count]
    row_start = row_joined[:, frame_count:]
    col_slopes = col_joined[:, :frame_count]
    col_start = col_joined[:, frame_count:]
    panel_width = col_start.shape[1]
    row_f = row_slopes.astype(jnp.float32)
    weight = damping / (jnp.sum(row_f * row_f, axis=1) / norm_count + noise)
    count = bands.shape[0]
    index = jnp.arange(count, dtype=jnp.int32)
    sym = jnp.where(index[:, None] <= index[None, :], bands, bands.T).astype(jnp.float32)
    row_ids = row_id * row_height + jnp.arange(row_height, dtype=jnp.int32)
    onehot = (row_ids[:, None] // SUBAP == index[None, :]).astype(jnp.float32)
    row_band = jnp.dot(onehot, sym, precision=lax.Precision.HIGHEST)
    row_pos = (row_ids % SUBAP).astype(jnp.float32)
    width = math.gcd(math.gcd(col_width, 512), SUBAP)
    nblocks = col_width // width

    def build(step, carry):
        tile, acc = carry
        offset = step * width
        cols = lax.dynamic_slice_in_dim(col_slopes, offset, width, 0)
        raw = (
            lax.dot_general(
                row_slopes, cols, (((1,), (1,)), ((), ())), preferred_element_type=jnp.float32
            )
            / norm_count
        )
        col_ids = col_id * col_width + offset + jnp.arange(width, dtype=jnp.int32)
        band = lax.dynamic_slice_in_dim(row_band, (col_id * col_width + offset) // SUBAP, 1, 1)
        dist = jnp.abs(row_pos[:, None] - (col_ids % SUBAP).astype(jnp.float32)[None, :])
        taper = jnp.maximum(0.0, 1.0 - dist / band)
        diag = jnp.where(row_ids[:, None] == col_ids[None, :], noise[:, None], jnp.float32(0.0))
        entry = (taper * raw + diag).astype(jnp.bfloat16)
        tile = lax.dynamic_update_slice_in_dim(tile, entry, offset, 1)
        return (tile, acc)

    tile_init = jnp.zeros((row_height, col_width), jnp.bfloat16)
    acc_init = jnp.zeros((row_height, panel_width), jnp.float32)
    tile, acc = lax.fori_loop(0, nblocks, build, (tile_init, acc_init))
    product0 = jnp.dot(tile, col_start, preferred_element_type=jnp.float32)
    target_f = target.astype(jnp.float32)

    def refine(current, product):
        share = lax.psum_scatter(product, "col", scatter_dimension=0, tiled=True)
        share_rows = row_height // col_count
        begin = col_id * share_rows
        cur_part = lax.dynamic_slice_in_dim(current, begin, share_rows, 0)
        tgt_part = lax.dynamic_slice_in_dim(target_f, begin, share_rows, 0)
        wgt_part = lax.dynamic_slice_in_dim(weight, begin, share_rows, 0)
        updated = cur_part + wgt_part[:, None] * (tgt_part - share)
        return lax.all_gather(updated, "col", axis=0, tiled=True)

    first = refine(row_start.astype(jnp.float32), product0)
    first_low = first.astype(jnp.bfloat16)
    pieces = [from_root(first_low, "row", col_id * ratio + offset_q) for offset_q in range(ratio)]
    col_first = jnp.concatenate(pieces, axis=0)
    product1 = jnp.dot(tile, col_first, preferred_element_type=jnp.float32)
    second = refine(first, product1)
    return (first, second)


EDGE = 256
STEP = 128
PAD = 384
ROUND = 4


def prepare_kernel(*refs):
    count = 6
    sources, (block, side, lent), copies = refs[:count], refs[count : count + 3], refs[count + 3 :]
    done = copies[count]
    moves = []
    for k in range(count):
        move = pltpu.make_async_copy(sources[k], copies[k], done.at[k])
        move.start()
        moves.append(move)
    for move in moves:
        move.wait()
    telemetry, scales, start, target, noise, bands = copies[:count]
    lent[...] = bands[...]
    panel, chunk = start.shape
    slopes = telemetry[...].astype(jnp.float32) * scales[...].astype(jnp.float32) / 128.0
    block[0:panel, :] = start[...]
    block[panel:, :] = slopes.astype(jnp.bfloat16)
    pieces = target.shape[1] // STEP
    for piece in range(pieces):
        part = slice(piece * STEP, (piece + 1) * STEP)
        side[piece * panel : (piece + 1) * panel, :] = target[:, part]
    rest = jnp.concatenate(
        [noise[:, piece * STEP : (piece + 1) * STEP] for piece in range(pieces)], axis=0
    )
    planes = []
    for _ in range(3):
        plane = rest.astype(jnp.bfloat16).astype(jnp.float32)
        rest = rest - plane
        planes.append(plane)
    planes.append(jnp.zeros_like(rest))
    side[pieces * panel :, :] = jnp.concatenate(planes, axis=0).astype(jnp.bfloat16)


def spot(row):
    return row + row // SUBAP * (2 * PAD) + PAD


def column(ref, begin, width, rows=slice(None)):
    return ref[rows, pl.ds(pl.multiple_of(begin, STEP), width)]


def moments(panel_ref, flat, sums):
    panel = 64
    local = (lax.broadcasted_iota(jnp.int32, (panel, STEP), 1) - STEP // 2).astype(jnp.float32)
    for sensor in range(sums.shape[0]):
        begins = [padded_start(sensor) + t * STEP for t in range(SUBAP // STEP)]
        dots = []
        for begin in begins:
            x = panel_ref[0:panel, begin : begin + STEP]
            xq = (x.astype(jnp.float32) * local).astype(jnp.bfloat16)
            dots.append(
                jnp.dot(
                    jnp.concatenate([x, xq], axis=0),
                    flat[begin : begin + STEP, :],
                    preferred_element_type=jnp.float32,
                )
            )
        plain = jnp.zeros((panel, 128), jnp.float32)
        moved = jnp.zeros((panel, 128), jnp.float32)
        for t, both in enumerate(dots):
            sums[sensor, t, 0:panel, :] = plain
            sums[sensor, t, panel:, :] = moved
            plain = plain + both[0:panel]
            moved = moved + (both[panel:] + both[0:panel] * float(t * STEP + STEP // 2))
        sums[sensor, SUBAP // STEP, 0:panel, :] = plain
        sums[sensor, SUBAP // STEP, panel:, :] = moved


def fill_ramp(ramp):
    rows = lax.broadcasted_iota(jnp.int32, ramp.shape, 0)
    cols = lax.broadcasted_iota(jnp.int32, ramp.shape, 1)
    ramp[...] = (rows - cols).astype(jnp.float32)


def taper_kernel(norm_count, bands, tapers, slants, ramp):
    fill_ramp(ramp)
    scale = 1.0 / norm_count
    sensors = tapers.shape[0]
    for a in range(sensors):
        for b in range(sensors):
            i, j = min(a, b), max(a, b)
            rate = 1.0 / bands[i : i + 1, j : j + 1].astype(jnp.float32)
            fall = jnp.broadcast_to(rate * scale, (1, EDGE))
            tapers[a, b] = jnp.maximum(0.0, scale - jnp.abs(ramp[0:EDGE, :]) * fall)
            slant = ramp[...] * fall
            slants[2 * (a * sensors + b)] = slant
            slants[2 * (a * sensors + b) + 1] = -slant


def padded_start(sensor):
    return sensor * (SUBAP + 2 * PAD) + PAD


def clear_pads(ref, axis, sensors):
    for sensor in range(sensors):
        for begin in (padded_start(sensor) - PAD, padded_start(sensor) + SUBAP):
            if axis:
                ref[:, begin : begin + PAD] = jnp.zeros((ref.shape[0], PAD), ref.dtype)
            else:
                ref[begin : begin + PAD, :] = jnp.zeros((PAD, ref.shape[1]), ref.dtype)


def keep_slopes(wide, base, height, own_slopes, at):
    panel = wide.shape[0] // 2
    own_slopes[0:panel, at : at + height] = jnp.zeros((panel, height), own_slopes.dtype)
    own_slopes[panel:, at : at + height] = column(wide, spot(base), height, slice(panel, None))


def edges(place, width):
    slim = (width & (STEP - 1)) == 0
    span = jnp.where(slim, EDGE, PAD)
    low = jnp.minimum((place - width) & -STEP, place - span)
    high = jnp.maximum((place + width) & -STEP, place + EDGE)
    return low, high, span, slim.astype(jnp.int32)


def widths(bands, sensor, sensors):
    return [bands[jnp.minimum(sensor, b), jnp.maximum(sensor, b)] for b in range(sensors)]


def list_jobs(bands, bases, height, sensors, jobs):
    number = [jnp.int32(0), jnp.int32(0)]
    for group, base in enumerate(bases):
        sensor = base // SUBAP
        for b, width in enumerate(widths(bands, sensor, sensors)):
            for k in range(height // EDGE):
                place = base - sensor * SUBAP + k * EDGE
                low, high, span, slim = edges(place, width)
                sides = ((low, low + span > 0), (high, high < SUBAP))
                for side, (begin, wanted) in enumerate(sides):
                    at = jnp.where(slim == 1, number[1], number[0])
                    jobs[slim, 0, at] = group * (height // EDGE) + k
                    jobs[slim, 1, at] = begin + padded_start(b)
                    jobs[slim, 2, at] = begin - place
                    jobs[slim, 3, at] = width
                    jobs[slim, 4, at] = 2 * (sensor * sensors + b) + side
                    one = wanted.astype(jnp.int32)
                    number = [number[0] + one * (1 - slim), number[1] + one * slim]
    for kind in range(2):
        for fill in range(ROUND - 1):
            for field, value in enumerate((0, 0, 0, 1, 0)):
                jobs[kind, field, number[kind] + fill] = value
    return [(count + (ROUND - 1)) // ROUND for count in number]


def near_and_far(
    base, group, norm_count, bands, panel_ref, flat, own_slopes, sums, tapers, ramp, noise, acc, saved, fresh
):
    panel = acc.shape[1]
    scale = 1.0 / norm_count
    sensors = sums.shape[0]
    sensor = base // SUBAP
    count = noise.shape[1] // EDGE
    local = (lax.broadcasted_iota(jnp.int32, (1, EDGE), 1) - EDGE // 2).astype(jnp.float32)
    width = widths(bands, sensor, sensors)
    rates = [1.0 / jnp.full((1, EDGE), w.astype(jnp.float32)) for w in width]
    places = [base - sensor * SUBAP + k * EDGE for k in range(count)]
    slopes = [column(own_slopes, (group * count + k) * EDGE, EDGE) for k in range(count)]
    begins = [[pl.multiple_of(padded_start(b) + p, STEP) for b in range(sensors)] for p in places]
    if fresh:
        raws = [
            jnp.dot(
                jnp.concatenate([flat[pl.ds(begin, EDGE), :] for begin in begins[k]], axis=0),
                slopes[k],
                preferred_element_type=jnp.float32,
            )
            for k in range(count)
        ]
    fars = []
    for k in range(count):
        near = jnp.zeros((panel, 128), jnp.float32)
        tilt = jnp.zeros((panel, 128), jnp.float32)
        middle = (places[k] + EDGE // 2).astype(jnp.float32)
        for b in range(sensors):
            low, high, span, _ = edges(places[k], width[b])
            rate = rates[b][:, 0:128]
            at = [
                jnp.maximum(low + span, 0) // STEP,
                places[k] // STEP,
                (places[k] + EDGE) // STEP,
                jnp.minimum(high, SUBAP) // STEP,
            ]
            zero = [sums[b, t, 0:panel, :] for t in at]
            one = [sums[b, t, panel:, :] for t in at]
            left, right = zero[1] - zero[0], zero[3] - zero[2]
            left_q, right_q = one[1] - one[0], one[3] - one[2]
            near += left + right + rate * ((left_q - middle * left) - (right_q - middle * right))
            tilt += rate * (right - left)
        mix = jnp.concatenate([near, tilt], axis=0) * scale
        mix_high = mix.astype(jnp.bfloat16)
        mix_low = (mix - mix_high.astype(jnp.float32)).astype(jnp.bfloat16)
        far = jnp.dot(
            jnp.concatenate([mix_high, mix_low], axis=0), slopes[k], preferred_element_type=jnp.float32
        )
        fars.append(far[0 : 2 * panel] + far[2 * panel :])
    entries = []
    if fresh:
        eye = ramp[0:STEP, 0:STEP] == 0.0
        for k in range(count):
            for b in range(sensors):
                same = (sensor == b).astype(jnp.float32)
                entry = tapers[sensor, b] * raws[k][b * EDGE : (b + 1) * EDGE]
                rows = []
                for r in range(EDGE // STEP):
                    part = slice(r * STEP, (r + 1) * STEP)
                    begin = k * EDGE + r * STEP
                    line = noise[:, begin : begin + STEP] * same
                    blocks = [entry[part, c * STEP : (c + 1) * STEP] for c in range(EDGE // STEP)]
                    blocks[r] = blocks[r] + jnp.where(eye, line, 0.0)
                    rows.append(jnp.concatenate(blocks, axis=1))
                entry = jnp.concatenate(rows, axis=0)
                entries.append(entry.astype(jnp.bfloat16))
                if saved is not None:
                    saved[k * sensors + b] = entries[-1]
    else:
        entries = [saved[n] for n in range(count * sensors)]
    for k in range(count):
        total = fars[k][0:panel] + local * fars[k][panel:]
        for b in range(sensors):
            total += jnp.dot(
                column(panel_ref, begins[k][b], EDGE, slice(0, panel)),
                entries[k * sensors + b],
                preferred_element_type=jnp.float32,
            )
        acc[group * count + k] = total


def run_jobs(rounds, norm_count, panel_ref, flat, own_slopes, slants, jobs, acc, saved, fresh):
    panel = acc.shape[1]
    scale = 1.0 / norm_count

    def body(kind, step):
        span = saved[kind].shape[1]
        kept = saved[kind].shape[0] - ROUND
        picked = [[jobs[kind, field, step * ROUND + u] for field in range(5)] for u in range(ROUND)]
        begins = [pl.multiple_of(job[1], STEP) for job in picked]
        if fresh:
            raws = [
                jnp.dot(
                    flat[pl.ds(begin, span), :],
                    column(own_slopes, job[0] * EDGE, EDGE),
                    preferred_element_type=jnp.float32,
                )
                for job, begin in zip(picked, begins)
            ]
            entries = []
            for u, ((tile, begin, gap, width, slant), raw) in enumerate(zip(picked, raws)):
                fall = scale / jnp.full((1, EDGE), width.astype(jnp.float32))
                top = scale - jnp.abs(gap).astype(jnp.float32) * fall
                taper = jnp.maximum(0.0, top + slants[slant, 0:span, :])
                entries.append((taper * raw).astype(jnp.bfloat16))
                saved[kind][jnp.minimum(step * ROUND, kept) + u] = entries[-1]
        else:
            entries = [saved[kind][step * ROUND + u] for u in range(ROUND)]
        parts = [
            jnp.dot(
                column(panel_ref, begin, span, slice(0, panel)), entry, preferred_element_type=jnp.float32
            )
            for begin, entry in zip(begins, entries)
        ]
        for job, part in zip(picked, parts):
            acc[job[0]] += part

    for kind in range(2):

        def step(count, _, kind=kind):
            body(kind, count)
            return 0

        lax.fori_loop(0, rounds[kind], step, 0)


def place_parts(sizes, parts, wide, flat):
    rows_n, cols_n, chunk, height, panel, norm_count, hops = sizes
    col_id, row_id = lax.axis_index("col"), lax.axis_index("row")
    core = row_id % 2
    own = row_id // 2
    starts = [spot((hop ^ col_id) * (rows_n * chunk)) for hop in hops]
    for j, near, source in parts:
        shift = (2 * (own ^ j) + (core if near else 1 - core)) * chunk
        for slot in range(cols_n):
            place = pl.multiple_of(starts[slot] + shift, STEP)
            part = source[slot * chunk : (slot + 1) * chunk, :]
            wide[:, pl.ds(place, chunk)] = part
            flat[pl.ds(place, chunk), :] = part.T


def place_kernel(sizes, which, fresh, *refs):
    count = len(which)
    wide, flat = refs[-2:]
    if fresh:
        sensors = wide.shape[1] // (SUBAP + 2 * PAD)
        clear_pads(wide, 1, sensors)
        clear_pads(flat, 0, sensors)
    sources = refs[len(refs) - 2 - count : len(refs) - 2]
    place_parts(sizes, [(j, near, source) for (j, near), source in zip(which, sources)], wide, flat)


def first_kernel(sizes, which, bands_in, *refs):
    rows_n, cols_n, chunk, height, panel, norm_count, hops = sizes
    half = rows_n // 2
    sources, sides = refs[2 : 2 + len(which)], refs[2 + len(which)]
    tapers, slants, ramp = refs[3 + len(which) : 6 + len(which)]
    refs = refs[6 + len(which) :]
    wide, flat, low, first, weight, saved_near, *saved_jobs = refs[:8]
    sums, noises, acc, own_slopes, bands, jobs, done = refs[8:]
    lend = pltpu.make_async_copy(bands_in, bands, done)
    lend.start()
    sensors = sums.shape[0]
    row_id = lax.axis_index("row")
    core = row_id % 2
    own = row_id // 2
    pieces = height // STEP
    per_side = pieces * panel + 16
    place_parts(sizes, [(j, near, source) for (j, near), source in zip(which, sources)], wide, flat)
    for j in range(half):
        planes = sides[(j + 1) * per_side - 16 : (j + 1) * per_side, :].astype(jnp.float32)
        lines = planes[0:pieces] + planes[pieces : 2 * pieces] + planes[2 * pieces : 3 * pieces]
        noises[j, 0:1, :] = jnp.concatenate([lines[t : t + 1] for t in range(pieces)], axis=1)
    moments(wide, flat, sums)
    bases = [(2 * (own ^ j) + core) * height for j in range(half)]
    for j in range(half):
        keep_slopes(wide, bases[j], height, own_slopes, j * height)
    lend.wait()

    for j in range(half):
        near_and_far(
            bases[j],
            j,
            norm_count,
            bands,
            wide,
            flat,
            own_slopes,
            sums,
            tapers,
            ramp,
            noises[j, 0:1, :],
            acc,
            saved_near if j == 0 else None,
            True,
        )
    rounds = list_jobs(bands, bases, height, sensors, jobs)
    run_jobs(rounds, norm_count, wide, flat, own_slopes, slants, jobs, acc, saved_jobs, True)
    for j in range(half):
        for k in range(height // EDGE):
            part = slice(k * EDGE, (k + 1) * EDGE)
            both = column(wide, spot(bases[j]) + k * EDGE, EDGE).astype(jnp.float32)
            power = jnp.sum(both[panel:] * both[panel:], axis=0, keepdims=True)
            wgt = damping / (power / norm_count + noises[j, 0:1, part])
            goal = jnp.concatenate(
                [
                    sides[j * per_side + t * panel : j * per_side + (t + 1) * panel, :]
                    for t in range(k * EDGE // STEP, (k + 1) * EDGE // STEP)
                ],
                axis=1,
            ).astype(jnp.float32)
            new = both[0:panel] + wgt * (goal - acc[j * (height // EDGE) + k])
            if j == 0:
                first[:, part] = new
                weight[:, part] = jnp.broadcast_to(wgt, (8, EDGE))
            into = pl.multiple_of((own ^ j) * height + k * EDGE, EDGE)
            low[:, pl.ds(into, EDGE)] = new.astype(jnp.bfloat16)


def second_kernel(sizes, bands_in, wide, flat, home, away, first, weight, target, *refs):
    saved_near, *saved_jobs = refs[:3]
    second, first_out, new, sums, acc, own_slopes, bands, jobs, done = refs[3:]
    rows_n, cols_n, chunk, height, panel, norm_count, hops = sizes
    lend = pltpu.make_async_copy(bands_in, bands, done.at[0])
    lend.start()
    give = pltpu.make_async_copy(first, first_out, done.at[1])
    give.start()
    sensors = sums.shape[0]
    row_id = lax.axis_index("row")
    core = row_id % 2
    clear_pads(new, 1, sensors)
    for pos in range(rows_n // 2):
        for source, parity in ((home, core), (away, 1 - core)):
            place = pl.multiple_of(spot((2 * pos + parity) * height), STEP)
            new[:, pl.ds(place, height)] = source[:, pos * height : (pos + 1) * height]
    moments(new, flat, sums)
    base = row_id * height
    keep_slopes(wide, base, height, own_slopes, 0)
    lend.wait()
    rounds = list_jobs(bands, [base], height, sensors, jobs)
    near_and_far(
        base, 0, norm_count, bands, new, flat, own_slopes, sums, None, None, weight, acc, saved_near, False
    )
    run_jobs(rounds, norm_count, new, flat, own_slopes, None, jobs, acc, saved_jobs, False)
    for k in range(height // EDGE):
        part = slice(k * EDGE, (k + 1) * EDGE)
        goal = target[:, part].astype(jnp.float32)
        second[:, part] = first[:, part] + weight[0:1, part] * (goal - acc[k])
    give.wait()


def flip(block, axis, bit):
    size = lax.axis_size(axis)
    return lax.ppermute(block, axis, [(i, i ^ bit) for i in range(size)])


def gathered_plan(telemetry, scales, bands, noise, start, target):
    rows_n = lax.axis_size("row")
    cols_n = lax.axis_size("col")
    chunk, frames = telemetry.shape
    height, panel = target.shape
    order = chunk * rows_n * cols_n
    sensors = order // SUBAP
    padded = order + 2 * PAD * sensors
    half = rows_n // 2
    vmem = pl.BlockSpec(memory_space=pltpu.VMEM)
    params = pltpu.CompilerParams(vmem_limit_bytes=24 * 1024 * 1024)
    noise = noise.reshape(1, height)
    target = target.T
    own = (telemetry.T, scales.reshape(1, chunk), start.T, target, noise, bands)
    block, side, bands = pl.pallas_call(
        prepare_kernel,
        out_shape=(
            jax.ShapeDtypeStruct((2 * panel, chunk), jnp.bfloat16),
            jax.ShapeDtypeStruct((height // STEP * panel + 16, 128), jnp.bfloat16),
            jax.ShapeDtypeStruct(bands.shape, bands.dtype),
        ),
        in_specs=[pl.BlockSpec(memory_space=pltpu.HBM)] * len(own),
        out_specs=(vmem,) * 3,
        scratch_shapes=[pltpu.VMEM(x.shape, x.dtype) for x in own]
        + [pltpu.SemaphoreType.DMA((len(own),))],
        compiler_params=params,
        name="prepare",
    )(*[pltpu.with_memory_space_constraint(x, pltpu.HBM) for x in own])
    shapes = pl.pallas_call(
        functools.partial(taper_kernel, float(order // 4)),
        out_shape=(
            jax.ShapeDtypeStruct((sensors, sensors, EDGE, EDGE), jnp.float32),
            jax.ShapeDtypeStruct((2 * sensors * sensors, PAD, EDGE), jnp.float32),
            jax.ShapeDtypeStruct((PAD, EDGE), jnp.float32),
        ),
        in_specs=[vmem],
        out_specs=(vmem,) * 3,
        compiler_params=params,
        name="tapers",
    )(bands)
    hops = (0,)
    bit = cols_n // 2
    while bit:
        block = jnp.concatenate([block, flip(block, "col", bit)], axis=0)
        hops = hops + tuple(hop ^ bit for hop in hops)
        bit //= 2
    bit = 2
    while bit < rows_n:
        side = jnp.concatenate([side, flip(side, "row", bit)], axis=0)
        bit *= 2
    sizes = (rows_n, cols_n, chunk, height, panel, float(order // 4), hops)
    mine = [block] + [flip(block, "row", 2 * j) for j in range(1, half)]
    other = [flip(part, "row", 1) for part in mine]
    tiles = height // EDGE
    sums = pltpu.VMEM((sensors, SUBAP // STEP + 1, 2 * panel, 128), jnp.float32)
    lent = pltpu.SMEM(bands.shape, bands.dtype)

    def scratch(groups):
        return [
            pltpu.VMEM((groups * tiles, panel, EDGE), jnp.float32),
            pltpu.VMEM((2 * panel, groups * height), jnp.bfloat16),
            lent,
            pltpu.SMEM((2, 5, groups * tiles * sensors * 2 + ROUND), jnp.int32),
        ]

    placed = (
        jax.ShapeDtypeStruct((2 * panel, padded), jnp.bfloat16),
        jax.ShapeDtypeStruct((padded, 2 * panel), jnp.bfloat16),
    )

    def place(which, before):
        parts = [mine[j] if near else other[j] for j, near in which]
        return pl.pallas_call(
            functools.partial(place_kernel, sizes, which, not before),
            out_shape=placed,
            in_specs=[vmem] * (len(before) + len(parts)),
            out_specs=(vmem,) * 2,
            input_output_aliases={k: k for k in range(len(before))},
            compiler_params=params,
            name="place",
        )(*before, *parts)

    everything = [(j, near) for j in range(half) for near in (True, False)]
    early = [[(0, True), (0, False)], [(1, True), (2, True), (3, True)]]
    arrays = ()
    for which in early:
        arrays = place(which, arrays)
    late = [pair for pair in everything if pair not in sum(early, [])]
    wide, flat, low, first, weight, *saved = pl.pallas_call(
        functools.partial(first_kernel, sizes, late),
        out_shape=placed
        + (
            jax.ShapeDtypeStruct((panel, half * height), jnp.bfloat16),
            jax.ShapeDtypeStruct((panel, height), jnp.float32),
            jax.ShapeDtypeStruct((8, height), jnp.float32),
            jax.ShapeDtypeStruct((tiles * sensors, EDGE, EDGE), jnp.bfloat16),
            jax.ShapeDtypeStruct((tiles * sensors * 2 + ROUND, PAD, EDGE), jnp.bfloat16),
            jax.ShapeDtypeStruct((tiles * sensors * 2 + ROUND, EDGE, EDGE), jnp.bfloat16),
        ),
        in_specs=[vmem] * (7 + len(late)),
        out_specs=(vmem,) * 8,
        input_output_aliases={1: 0, 2: 1},
        scratch_shapes=[sums, pltpu.VMEM((half, 8, height), jnp.float32)]
        + scratch(half)
        + [pltpu.SemaphoreType.DMA],
        compiler_params=params,
        name="first_pass",
    )(bands, *arrays, *[mine[j] if near else other[j] for j, near in late], side, *shapes)
    away = flip(low, "row", 1)
    second, first = pl.pallas_call(
        functools.partial(second_kernel, sizes),
        out_shape=(jax.ShapeDtypeStruct((panel, height), jnp.float32),) * 2,
        in_specs=[vmem] * 11,
        out_specs=(vmem, pl.BlockSpec(memory_space=pl.ANY)),
        scratch_shapes=[pltpu.VMEM((panel, padded), jnp.bfloat16), sums]
        + scratch(1)
        + [pltpu.SemaphoreType.DMA((2,))],
        compiler_params=params,
        name="second_pass",
    )(bands, wide, flat, low, away, first, weight, target, *saved)
    return (first.T, second.T)


def power_of_two(number):
    return number > 0 and number & (number - 1) == 0


def fits(mesh, telemetry, target):
    rows_n, cols_n = mesh.shape["row"], mesh.shape["col"]
    order, frames = telemetry.shape
    panel = target.shape[1]
    height = order // rows_n
    return (
        power_of_two(rows_n)
        and power_of_two(cols_n)
        and rows_n >= 2
        and frames == panel == 64
        and order % SUBAP == 0
        and SUBAP % height == 0
        and height == 2 * EDGE
        and order // (rows_n * cols_n) == STEP
        and order <= 2 * SUBAP
    )


def solution(mesh):
    def program(telemetry, scales, bands, noise, start, target):
        plan = gathered_plan if fits(mesh, telemetry, target) else tiled_plan
        return jax.shard_map(
            plan,
            mesh=mesh,
            in_specs=(
                P(("col", "row"), None),
                P(("col", "row")),
                P(),
                P("row"),
                P(("col", "row"), None),
                P("row", None),
            ),
            out_specs=(P("row", None), P("row", None)),
            check_vma=False,
        )(telemetry, scales, bands, noise, start, target)

    return program
```

```python
import functools
import math

import jax
import jax.numpy as jnp
from jax import lax
from jax.experimental import pallas as pl
from jax.experimental.pallas import tpu as pltpu
from jax.sharding import PartitionSpec as P

SUBAP = 2048


damping = 0.4


def from_root(block, axis, holder):
    block = jnp.where(lax.axis_index(axis) == holder, block, jnp.zeros_like(block))
    return lax.psum(block, axis)


def tiled_plan(telemetry, scales, bands, noise, start, target):
    frame_count = telemetry.shape[1]
    row_count = lax.axis_size("row")
    col_count = lax.axis_size("col")
    ratio = row_count // col_count
    row_id = lax.axis_index("row")
    col_id = lax.axis_index("col")
    order_total = telemetry.shape[0] * row_count * col_count
    norm_count = jnp.float32(order_total // 4)
    slopes = (telemetry.astype(jnp.float32) * scales.astype(jnp.float32)[:, None] / 128.0).astype(
        jnp.bfloat16
    )
    joined = jnp.concatenate([slopes, start], axis=1)
    col_joined = lax.all_gather(joined, "row", axis=0, tiled=True)
    col_width = col_joined.shape[0]
    row_height = col_width // ratio
    half = lax.dynamic_slice_in_dim(col_joined, row_id % ratio * row_height, row_height, 0)
    row_joined = from_root(half, "col", row_id // ratio)
    row_slopes = row_joined[:, :frame_count]
    row_start = row_joined[:, frame_count:]
    col_slopes = col_joined[:, :frame_count]
    col_start = col_joined[:, frame_count:]
    panel_width = col_start.shape[1]
    row_f = row_slopes.astype(jnp.float32)
    weight = damping / (jnp.sum(row_f * row_f, axis=1) / norm_count + noise)
    count = bands.shape[0]
    index = jnp.arange(count, dtype=jnp.int32)
    sym = jnp.where(index[:, None] <= index[None, :], bands, bands.T).astype(jnp.float32)
    row_ids = row_id * row_height + jnp.arange(row_height, dtype=jnp.int32)
    onehot = (row_ids[:, None] // SUBAP == index[None, :]).astype(jnp.float32)
    row_band = jnp.dot(onehot, sym, precision=lax.Precision.HIGHEST)
    row_pos = (row_ids % SUBAP).astype(jnp.float32)
    width = math.gcd(math.gcd(col_width, 512), SUBAP)
    nblocks = col_width // width

    def build(step, carry):
        tile, acc = carry
        offset = step * width
        cols = lax.dynamic_slice_in_dim(col_slopes, offset, width, 0)
        raw = (
            lax.dot_general(
                row_slopes, cols, (((1,), (1,)), ((), ())), preferred_element_type=jnp.float32
            )
            / norm_count
        )
        col_ids = col_id * col_width + offset + jnp.arange(width, dtype=jnp.int32)
        band = lax.dynamic_slice_in_dim(row_band, (col_id * col_width + offset) // SUBAP, 1, 1)
        dist = jnp.abs(row_pos[:, None] - (col_ids % SUBAP).astype(jnp.float32)[None, :])
        taper = jnp.maximum(0.0, 1.0 - dist / band)
        diag = jnp.where(row_ids[:, None] == col_ids[None, :], noise[:, None], jnp.float32(0.0))
        entry = (taper * raw + diag).astype(jnp.bfloat16)
        tile = lax.dynamic_update_slice_in_dim(tile, entry, offset, 1)
        return (tile, acc)

    tile_init = jnp.zeros((row_height, col_width), jnp.bfloat16)
    acc_init = jnp.zeros((row_height, panel_width), jnp.float32)
    tile, acc = lax.fori_loop(0, nblocks, build, (tile_init, acc_init))
    product0 = jnp.dot(tile, col_start, preferred_element_type=jnp.float32)
    target_f = target.astype(jnp.float32)

    def refine(current, product):
        share = lax.psum_scatter(product, "col", scatter_dimension=0, tiled=True)
        share_rows = row_height // col_count
        begin = col_id * share_rows
        cur_part = lax.dynamic_slice_in_dim(current, begin, share_rows, 0)
        tgt_part = lax.dynamic_slice_in_dim(target_f, begin, share_rows, 0)
        wgt_part = lax.dynamic_slice_in_dim(weight, begin, share_rows, 0)
        updated = cur_part + wgt_part[:, None] * (tgt_part - share)
        return lax.all_gather(updated, "col", axis=0, tiled=True)

    first = refine(row_start.astype(jnp.float32), product0)
    first_low = first.astype(jnp.bfloat16)
    pieces = [from_root(first_low, "row", col_id * ratio + offset_q) for offset_q in range(ratio)]
    col_first = jnp.concatenate(pieces, axis=0)
    product1 = jnp.dot(tile, col_first, preferred_element_type=jnp.float32)
    second = refine(first, product1)
    return (first, second)


EDGE = 256
STEP = 128
PAD = 384
ROUND = 6


def prepare_kernel(*refs):
    count = 6
    sources, (block, side, lent), copies = refs[:count], refs[count : count + 3], refs[count + 3 :]
    done = copies[count]
    moves = []
    for k in range(count):
        move = pltpu.make_async_copy(sources[k], copies[k], done.at[k])
        move.start()
        moves.append(move)
    for move in moves:
        move.wait()
    telemetry, scales, start, target, noise, bands = copies[:count]
    lent[...] = bands[...]
    panel, chunk = start.shape
    slopes = telemetry[...].astype(jnp.float32) * scales[...].astype(jnp.float32) / 128.0
    block[0:panel, :] = start[...]
    block[panel:, :] = slopes.astype(jnp.bfloat16)
    pieces = target.shape[1] // STEP
    for piece in range(pieces):
        part = slice(piece * STEP, (piece + 1) * STEP)
        side[piece * panel : (piece + 1) * panel, :] = target[:, part]
    rest = jnp.concatenate(
        [noise[:, piece * STEP : (piece + 1) * STEP] for piece in range(pieces)], axis=0
    )
    planes = []
    for _ in range(3):
        plane = rest.astype(jnp.bfloat16).astype(jnp.float32)
        rest = rest - plane
        planes.append(plane)
    planes.append(jnp.zeros_like(rest))
    side[pieces * panel :, :] = jnp.concatenate(planes, axis=0).astype(jnp.bfloat16)


def spot(row):
    return row + row // SUBAP * (2 * PAD) + PAD


def column(ref, begin, width, rows=slice(None)):
    return ref[rows, pl.ds(pl.multiple_of(begin, STEP), width)]


def moments(panel_ref, flat, sums):
    panel = 64
    local = (lax.broadcasted_iota(jnp.int32, (panel, STEP), 1) - STEP // 2).astype(jnp.float32)
    for sensor in range(sums.shape[0]):
        begins = [padded_start(sensor) + t * STEP for t in range(SUBAP // STEP)]
        dots = []
        for begin in begins:
            x = panel_ref[0:panel, begin : begin + STEP]
            xq = (x.astype(jnp.float32) * local).astype(jnp.bfloat16)
            dots.append(
                jnp.dot(
                    jnp.concatenate([x, xq], axis=0),
                    flat[begin : begin + STEP, :],
                    preferred_element_type=jnp.float32,
                )
            )
        plain = jnp.zeros((panel, 128), jnp.float32)
        moved = jnp.zeros((panel, 128), jnp.float32)
        for t, both in enumerate(dots):
            sums[sensor, t, 0:panel, :] = plain
            sums[sensor, t, panel:, :] = moved
            plain = plain + both[0:panel]
            moved = moved + (both[panel:] + both[0:panel] * float(t * STEP + STEP // 2))
        sums[sensor, SUBAP // STEP, 0:panel, :] = plain
        sums[sensor, SUBAP // STEP, panel:, :] = moved


def fill_ramp(ramp):
    rows = lax.broadcasted_iota(jnp.int32, ramp.shape, 0)
    cols = lax.broadcasted_iota(jnp.int32, ramp.shape, 1)
    ramp[...] = (rows - cols).astype(jnp.float32)


def taper_kernel(norm_count, bands, tapers, slants, ramp):
    fill_ramp(ramp)
    scale = 1.0 / norm_count
    sensors = tapers.shape[0]
    for a in range(sensors):
        for b in range(sensors):
            i, j = min(a, b), max(a, b)
            rate = 1.0 / bands[i : i + 1, j : j + 1].astype(jnp.float32)
            fall = jnp.broadcast_to(rate * scale, (1, EDGE))
            tapers[a, b] = jnp.maximum(0.0, scale - jnp.abs(ramp[0:EDGE, :]) * fall)
            slant = ramp[...] * fall
            slants[2 * (a * sensors + b)] = slant
            slants[2 * (a * sensors + b) + 1] = -slant


def padded_start(sensor):
    return sensor * (SUBAP + 2 * PAD) + PAD


def clear_pads(ref, axis, sensors):
    for sensor in range(sensors):
        for begin in (padded_start(sensor) - PAD, padded_start(sensor) + SUBAP):
            if axis:
                ref[:, begin : begin + PAD] = jnp.zeros((ref.shape[0], PAD), ref.dtype)
            else:
                ref[begin : begin + PAD, :] = jnp.zeros((PAD, ref.shape[1]), ref.dtype)


def keep_slopes(wide, base, height, own_slopes, at):
    panel = wide.shape[0] // 2
    own_slopes[0:panel, at : at + height] = jnp.zeros((panel, height), own_slopes.dtype)
    own_slopes[panel:, at : at + height] = column(wide, spot(base), height, slice(panel, None))


def edges(place, width):
    slim = (width & (STEP - 1)) == 0
    span = jnp.where(slim, EDGE, PAD)
    low = jnp.minimum((place - width) & -STEP, place - span)
    high = jnp.maximum((place + width) & -STEP, place + EDGE)
    return low, high, span, slim.astype(jnp.int32)


def widths(bands, sensor, sensors):
    return [bands[jnp.minimum(sensor, b), jnp.maximum(sensor, b)] for b in range(sensors)]


def list_jobs(bands, bases, height, sensors, jobs):
    number = [jnp.int32(0), jnp.int32(0)]
    for group, base in enumerate(bases):
        sensor = base // SUBAP
        for b, width in enumerate(widths(bands, sensor, sensors)):
            for k in range(height // EDGE):
                place = base - sensor * SUBAP + k * EDGE
                low, high, span, slim = edges(place, width)
                sides = ((low, low + span > 0), (high, high < SUBAP))
                for side, (begin, wanted) in enumerate(sides):
                    at = jnp.where(slim == 1, number[1], number[0])
                    jobs[slim, 0, at] = group * (height // EDGE) + k
                    jobs[slim, 1, at] = begin + padded_start(b)
                    jobs[slim, 2, at] = begin - place
                    jobs[slim, 3, at] = width
                    jobs[slim, 4, at] = 2 * (sensor * sensors + b) + side
                    one = wanted.astype(jnp.int32)
                    number = [number[0] + one * (1 - slim), number[1] + one * slim]
    for kind in range(2):
        for fill in range(ROUND - 1):
            for field, value in enumerate((0, 0, 0, 1, 0)):
                jobs[kind, field, number[kind] + fill] = value
    return [(count + (ROUND - 1)) // ROUND for count in number]


def near_and_far(
    base, group, norm_count, bands, panel_ref, flat, own_slopes, sums, tapers, ramp, noise, acc, saved, fresh
):
    panel = acc.shape[1]
    scale = 1.0 / norm_count
    sensors = sums.shape[0]
    sensor = base // SUBAP
    count = noise.shape[1] // EDGE
    local = (lax.broadcasted_iota(jnp.int32, (1, EDGE), 1) - EDGE // 2).astype(jnp.float32)
    width = widths(bands, sensor, sensors)
    rates = [1.0 / jnp.full((1, EDGE), w.astype(jnp.float32)) for w in width]
    places = [base - sensor * SUBAP + k * EDGE for k in range(count)]
    slopes = [column(own_slopes, (group * count + k) * EDGE, EDGE) for k in range(count)]
    begins = [[pl.multiple_of(padded_start(b) + p, STEP) for b in range(sensors)] for p in places]
    if fresh:
        raws = [
            jnp.dot(
                jnp.concatenate([flat[pl.ds(begin, EDGE), :] for begin in begins[k]], axis=0),
                slopes[k],
                preferred_element_type=jnp.float32,
            )
            for k in range(count)
        ]
    fars = []
    for k in range(count):
        near = jnp.zeros((panel, 128), jnp.float32)
        tilt = jnp.zeros((panel, 128), jnp.float32)
        middle = (places[k] + EDGE // 2).astype(jnp.float32)
        for b in range(sensors):
            low, high, span, _ = edges(places[k], width[b])
            rate = rates[b][:, 0:128]
            at = [
                jnp.maximum(low + span, 0) // STEP,
                places[k] // STEP,
                (places[k] + EDGE) // STEP,
                jnp.minimum(high, SUBAP) // STEP,
            ]
            zero = [sums[b, t, 0:panel, :] for t in at]
            one = [sums[b, t, panel:, :] for t in at]
            left, right = zero[1] - zero[0], zero[3] - zero[2]
            left_q, right_q = one[1] - one[0], one[3] - one[2]
            near += left + right + rate * ((left_q - middle * left) - (right_q - middle * right))
            tilt += rate * (right - left)
        mix = jnp.concatenate([near, tilt], axis=0) * scale
        mix_high = mix.astype(jnp.bfloat16)
        mix_low = (mix - mix_high.astype(jnp.float32)).astype(jnp.bfloat16)
        far = jnp.dot(
            jnp.concatenate([mix_high, mix_low], axis=0), slopes[k], preferred_element_type=jnp.float32
        )
        fars.append(far[0 : 2 * panel] + far[2 * panel :])
    entries = []
    if fresh:
        eye = ramp[0:STEP, 0:STEP] == 0.0
        for k in range(count):
            for b in range(sensors):
                same = (sensor == b).astype(jnp.float32)
                entry = tapers[sensor, b] * raws[k][b * EDGE : (b + 1) * EDGE]
                rows = []
                for r in range(EDGE // STEP):
                    part = slice(r * STEP, (r + 1) * STEP)
                    begin = k * EDGE + r * STEP
                    line = noise[:, begin : begin + STEP] * same
                    blocks = [entry[part, c * STEP : (c + 1) * STEP] for c in range(EDGE // STEP)]
                    blocks[r] = blocks[r] + jnp.where(eye, line, 0.0)
                    rows.append(jnp.concatenate(blocks, axis=1))
                entry = jnp.concatenate(rows, axis=0)
                entries.append(entry.astype(jnp.bfloat16))
                if saved is not None:
                    saved[k * sensors + b] = entries[-1]
    else:
        entries = [saved[n] for n in range(count * sensors)]
    for k in range(count):
        total = fars[k][0:panel] + local * fars[k][panel:]
        for b in range(sensors):
            total += jnp.dot(
                column(panel_ref, begins[k][b], EDGE, slice(0, panel)),
                entries[k * sensors + b],
                preferred_element_type=jnp.float32,
            )
        acc[group * count + k] = total


def run_jobs(rounds, norm_count, panel_ref, flat, own_slopes, slants, jobs, acc, saved, fresh):
    panel = acc.shape[1]
    scale = 1.0 / norm_count

    def body(kind, step):
        span = saved[kind].shape[1]
        kept = saved[kind].shape[0] - ROUND
        picked = [[jobs[kind, field, step * ROUND + u] for field in range(5)] for u in range(ROUND)]
        begins = [pl.multiple_of(job[1], STEP) for job in picked]
        if fresh:
            raws = [
                jnp.dot(
                    flat[pl.ds(begin, span), :],
                    column(own_slopes, job[0] * EDGE, EDGE),
                    preferred_element_type=jnp.float32,
                )
                for job, begin in zip(picked, begins)
            ]
            entries = []
            for u, ((tile, begin, gap, width, slant), raw) in enumerate(zip(picked, raws)):
                fall = scale / jnp.full((1, EDGE), width.astype(jnp.float32))
                top = scale - jnp.abs(gap).astype(jnp.float32) * fall
                taper = jnp.maximum(0.0, top + slants[slant, 0:span, :])
                entries.append((taper * raw).astype(jnp.bfloat16))
                saved[kind][jnp.minimum(step * ROUND, kept) + u] = entries[-1]
        else:
            entries = [saved[kind][step * ROUND + u] for u in range(ROUND)]
        parts = [
            jnp.dot(
                column(panel_ref, begin, span, slice(0, panel)), entry, preferred_element_type=jnp.float32
            )
            for begin, entry in zip(begins, entries)
        ]
        for job, part in zip(picked, parts):
            acc[job[0]] += part

    for kind in range(2):

        def step(count, _, kind=kind):
            body(kind, count)
            return 0

        lax.fori_loop(0, rounds[kind], step, 0)


def place_parts(sizes, parts, wide, flat):
    rows_n, cols_n, chunk, height, panel, norm_count, hops = sizes
    col_id, row_id = lax.axis_index("col"), lax.axis_index("row")
    core = row_id % 2
    own = row_id // 2
    starts = [spot((hop ^ col_id) * (rows_n * chunk)) for hop in hops]
    for j, near, source in parts:
        shift = (2 * (own ^ j) + (core if near else 1 - core)) * chunk
        for slot in range(cols_n):
            place = pl.multiple_of(starts[slot] + shift, STEP)
            part = source[slot * chunk : (slot + 1) * chunk, :]
            wide[:, pl.ds(place, chunk)] = part
            flat[pl.ds(place, chunk), :] = part.T


def place_kernel(sizes, which, fresh, *refs):
    count = len(which)
    wide, flat = refs[-2:]
    if fresh:
        sensors = wide.shape[1] // (SUBAP + 2 * PAD)
        clear_pads(wide, 1, sensors)
        clear_pads(flat, 0, sensors)
    sources = refs[len(refs) - 2 - count : len(refs) - 2]
    place_parts(sizes, [(j, near, source) for (j, near), source in zip(which, sources)], wide, flat)


def first_kernel(sizes, which, bands_in, *refs):
    rows_n, cols_n, chunk, height, panel, norm_count, hops = sizes
    half = rows_n // 2
    sources, sides = refs[2 : 2 + len(which)], refs[2 + len(which)]
    tapers, slants, ramp = refs[3 + len(which) : 6 + len(which)]
    refs = refs[6 + len(which) :]
    wide, flat, low, first, weight, saved_near, *saved_jobs = refs[:8]
    sums, noises, acc, own_slopes, bands, jobs, done = refs[8:]
    lend = pltpu.make_async_copy(bands_in, bands, done)
    lend.start()
    sensors = sums.shape[0]
    row_id = lax.axis_index("row")
    core = row_id % 2
    own = row_id // 2
    pieces = height // STEP
    per_side = pieces * panel + 16
    place_parts(sizes, [(j, near, source) for (j, near), source in zip(which, sources)], wide, flat)
    for j in range(half):
        planes = sides[(j + 1) * per_side - 16 : (j + 1) * per_side, :].astype(jnp.float32)
        lines = planes[0:pieces] + planes[pieces : 2 * pieces] + planes[2 * pieces : 3 * pieces]
        noises[j, 0:1, :] = jnp.concatenate([lines[t : t + 1] for t in range(pieces)], axis=1)
    moments(wide, flat, sums)
    bases = [(2 * (own ^ j) + core) * height for j in range(half)]
    for j in range(half):
        keep_slopes(wide, bases[j], height, own_slopes, j * height)
    lend.wait()

    for j in range(half):
        near_and_far(
            bases[j],
            j,
            norm_count,
            bands,
            wide,
            flat,
            own_slopes,
            sums,
            tapers,
            ramp,
            noises[j, 0:1, :],
            acc,
            saved_near if j == 0 else None,
            True,
        )
    rounds = list_jobs(bands, bases, height, sensors, jobs)
    run_jobs(rounds, norm_count, wide, flat, own_slopes, slants, jobs, acc, saved_jobs, True)
    for j in range(half):
        for k in range(height // EDGE):
            part = slice(k * EDGE, (k + 1) * EDGE)
            both = column(wide, spot(bases[j]) + k * EDGE, EDGE).astype(jnp.float32)
            power = jnp.sum(both[panel:] * both[panel:], axis=0, keepdims=True)
            wgt = damping / (power / norm_count + noises[j, 0:1, part])
            goal = jnp.concatenate(
                [
                    sides[j * per_side + t * panel : j * per_side + (t + 1) * panel, :]
                    for t in range(k * EDGE // STEP, (k + 1) * EDGE // STEP)
                ],
                axis=1,
            ).astype(jnp.float32)
            new = both[0:panel] + wgt * (goal - acc[j * (height // EDGE) + k])
            if j == 0:
                first[:, part] = new
                weight[:, part] = jnp.broadcast_to(wgt, (8, EDGE))
            into = pl.multiple_of((own ^ j) * height + k * EDGE, EDGE)
            low[:, pl.ds(into, EDGE)] = new.astype(jnp.bfloat16)


def second_kernel(sizes, bands_in, wide, flat, home, away, first, weight, target, *refs):
    saved_near, *saved_jobs = refs[:3]
    second, first_out, new, sums, acc, own_slopes, bands, jobs, done = refs[3:]
    rows_n, cols_n, chunk, height, panel, norm_count, hops = sizes
    lend = pltpu.make_async_copy(bands_in, bands, done.at[0])
    lend.start()
    give = pltpu.make_async_copy(first, first_out, done.at[1])
    give.start()
    sensors = sums.shape[0]
    row_id = lax.axis_index("row")
    core = row_id % 2
    clear_pads(new, 1, sensors)
    for pos in range(rows_n // 2):
        for source, parity in ((home, core), (away, 1 - core)):
            place = pl.multiple_of(spot((2 * pos + parity) * height), STEP)
            new[:, pl.ds(place, height)] = source[:, pos * height : (pos + 1) * height]
    moments(new, flat, sums)
    base = row_id * height
    keep_slopes(wide, base, height, own_slopes, 0)
    lend.wait()
    rounds = list_jobs(bands, [base], height, sensors, jobs)
    near_and_far(
        base, 0, norm_count, bands, new, flat, own_slopes, sums, None, None, weight, acc, saved_near, False
    )
    run_jobs(rounds, norm_count, new, flat, own_slopes, None, jobs, acc, saved_jobs, False)
    for k in range(height // EDGE):
        part = slice(k * EDGE, (k + 1) * EDGE)
        goal = target[:, part].astype(jnp.float32)
        second[:, part] = first[:, part] + weight[0:1, part] * (goal - acc[k])
    give.wait()


def flip(block, axis, bit):
    size = lax.axis_size(axis)
    return lax.ppermute(block, axis, [(i, i ^ bit) for i in range(size)])


def gathered_plan(telemetry, scales, bands, noise, start, target):
    rows_n = lax.axis_size("row")
    cols_n = lax.axis_size("col")
    chunk, frames = telemetry.shape
    height, panel = target.shape
    order = chunk * rows_n * cols_n
    sensors = order // SUBAP
    padded = order + 2 * PAD * sensors
    half = rows_n // 2
    vmem = pl.BlockSpec(memory_space=pltpu.VMEM)
    params = pltpu.CompilerParams(vmem_limit_bytes=24 * 1024 * 1024)
    noise = noise.reshape(1, height)
    target = target.T
    own = (telemetry.T, scales.reshape(1, chunk), start.T, target, noise, bands)
    block, side, bands = pl.pallas_call(
        prepare_kernel,
        out_shape=(
            jax.ShapeDtypeStruct((2 * panel, chunk), jnp.bfloat16),
            jax.ShapeDtypeStruct((height // STEP * panel + 16, 128), jnp.bfloat16),
            jax.ShapeDtypeStruct(bands.shape, bands.dtype),
        ),
        in_specs=[pl.BlockSpec(memory_space=pltpu.HBM)] * len(own),
        out_specs=(vmem,) * 3,
        scratch_shapes=[pltpu.VMEM(x.shape, x.dtype) for x in own]
        + [pltpu.SemaphoreType.DMA((len(own),))],
        compiler_params=params,
        name="prepare",
    )(*[pltpu.with_memory_space_constraint(x, pltpu.HBM) for x in own])
    shapes = pl.pallas_call(
        functools.partial(taper_kernel, float(order // 4)),
        out_shape=(
            jax.ShapeDtypeStruct((sensors, sensors, EDGE, EDGE), jnp.float32),
            jax.ShapeDtypeStruct((2 * sensors * sensors, PAD, EDGE), jnp.float32),
            jax.ShapeDtypeStruct((PAD, EDGE), jnp.float32),
        ),
        in_specs=[vmem],
        out_specs=(vmem,) * 3,
        compiler_params=params,
        name="tapers",
    )(bands)
    hops = (0,)
    bit = cols_n // 2
    while bit:
        block = jnp.concatenate([block, flip(block, "col", bit)], axis=0)
        hops = hops + tuple(hop ^ bit for hop in hops)
        bit //= 2
    bit = 2
    while bit < rows_n:
        side = jnp.concatenate([side, flip(side, "row", bit)], axis=0)
        bit *= 2
    sizes = (rows_n, cols_n, chunk, height, panel, float(order // 4), hops)
    mine = [block] + [flip(block, "row", 2 * j) for j in range(1, half)]
    other = [flip(part, "row", 1) for part in mine]
    tiles = height // EDGE
    sums = pltpu.VMEM((sensors, SUBAP // STEP + 1, 2 * panel, 128), jnp.float32)
    lent = pltpu.SMEM(bands.shape, bands.dtype)

    def scratch(groups):
        return [
            pltpu.VMEM((groups * tiles, panel, EDGE), jnp.float32),
            pltpu.VMEM((2 * panel, groups * height), jnp.bfloat16),
            lent,
            pltpu.SMEM((2, 5, groups * tiles * sensors * 2 + ROUND), jnp.int32),
        ]

    placed = (
        jax.ShapeDtypeStruct((2 * panel, padded), jnp.bfloat16),
        jax.ShapeDtypeStruct((padded, 2 * panel), jnp.bfloat16),
    )

    def place(which, before):
        parts = [mine[j] if near else other[j] for j, near in which]
        return pl.pallas_call(
            functools.partial(place_kernel, sizes, which, not before),
            out_shape=placed,
            in_specs=[vmem] * (len(before) + len(parts)),
            out_specs=(vmem,) * 2,
            input_output_aliases={k: k for k in range(len(before))},
            compiler_params=params,
            name="place",
        )(*before, *parts)

    everything = [(j, near) for j in range(half) for near in (True, False)]
    early = [[(0, True), (0, False)], [(1, True), (2, True), (3, True)]]
    arrays = ()
    for which in early:
        arrays = place(which, arrays)
    late = [pair for pair in everything if pair not in sum(early, [])]
    wide, flat, low, first, weight, *saved = pl.pallas_call(
        functools.partial(first_kernel, sizes, late),
        out_shape=placed
        + (
            jax.ShapeDtypeStruct((panel, half * height), jnp.bfloat16),
            jax.ShapeDtypeStruct((panel, height), jnp.float32),
            jax.ShapeDtypeStruct((8, height), jnp.float32),
            jax.ShapeDtypeStruct((tiles * sensors, EDGE, EDGE), jnp.bfloat16),
            jax.ShapeDtypeStruct((tiles * sensors * 2 + ROUND, PAD, EDGE), jnp.bfloat16),
            jax.ShapeDtypeStruct((tiles * sensors * 2 + ROUND, EDGE, EDGE), jnp.bfloat16),
        ),
        in_specs=[vmem] * (7 + len(late)),
        out_specs=(vmem,) * 8,
        input_output_aliases={1: 0, 2: 1},
        scratch_shapes=[sums, pltpu.VMEM((half, 8, height), jnp.float32)]
        + scratch(half)
        + [pltpu.SemaphoreType.DMA],
        compiler_params=params,
        name="first_pass",
    )(bands, *arrays, *[mine[j] if near else other[j] for j, near in late], side, *shapes)
    away = flip(low, "row", 1)
    second, first = pl.pallas_call(
        functools.partial(second_kernel, sizes),
        out_shape=(jax.ShapeDtypeStruct((panel, height), jnp.float32),) * 2,
        in_specs=[vmem] * 11,
        out_specs=(vmem, pl.BlockSpec(memory_space=pl.ANY)),
        scratch_shapes=[pltpu.VMEM((panel, padded), jnp.bfloat16), sums]
        + scratch(1)
        + [pltpu.SemaphoreType.DMA((2,))],
        compiler_params=params,
        name="second_pass",
    )(bands, wide, flat, low, away, first, weight, target, *saved)
    return (first.T, second.T)


def power_of_two(number):
    return number > 0 and number & (number - 1) == 0


def fits(mesh, telemetry, target):
    rows_n, cols_n = mesh.shape["row"], mesh.shape["col"]
    order, frames = telemetry.shape
    panel = target.shape[1]
    height = order // rows_n
    return (
        power_of_two(rows_n)
        and power_of_two(cols_n)
        and rows_n >= 2
        and frames == panel == 64
        and order % SUBAP == 0
        and SUBAP % height == 0
        and height == 2 * EDGE
        and order // (rows_n * cols_n) == STEP
        and order <= 2 * SUBAP
    )


def solution(mesh):
    def program(telemetry, scales, bands, noise, start, target):
        plan = gathered_plan if fits(mesh, telemetry, target) else tiled_plan
        return jax.shard_map(
            plan,
            mesh=mesh,
            in_specs=(
                P(("col", "row"), None),
                P(("col", "row")),
                P(),
                P("row"),
                P(("col", "row"), None),
                P("row", None),
            ),
            out_specs=(P("row", None), P("row", None)),
            check_vma=False,
        )(telemetry, scales, bands, noise, start, target)

    return program
```
